512 devices in a mesh: dp: 4 (over y), emb: 128 (over x, z, core).
Axes of the slice: x: 4, y: 4, z: 16, core: 2. Of those that a mesh axis runs over, the one named last changes fastest.
Arguments:
- history: bfloat16 [512, 256, 512], P(('dp', 'emb')), may hold values from -6 to 6
- dout: bfloat16 [512, 256, 512], P(('dp', 'emb')), may hold values from -6 to 6
- lengths: int32 [512], P(('dp', 'emb')), may hold values from 1 to 256, 65536 in all
- item_ids: int32 [512, 256], P(('dp', 'emb')), may hold values from 0 to 32767, as said below
- row_place: int32 [32768], replicated, may hold values from 0 to 32767, as said below
- w1: bfloat16 [2048, 512], replicated, may hold values from -0.25 to 0.25
Outputs:
- table_grad: float32 [32768, 512], P('emb')
- weight_grad: float32 [2048, 512], P(('dp', 'emb'))
The draws below stay inside these ranges and needn't reach their ends.
Inputs may be any that keep to these rules, and one draw needn't show every extreme that they name: `row_place`: A permutation of the table rows. `item_ids`: among the positions of one device's users, at most 4 name rows placed on any one shard; in every draw some shard gets exactly 4 from every device.
All inputs are finite; a program needn't handle non-finite values. No bound on the sum of `lengths` on one device may be relied on, other than what follows from the above.
Results may differ from the reference program's by a relative error of at most 0.0085.
Values may be sent and summed in bfloat16 or wider, within the bound.
A program may use at most 64 MiB of HBM per device.

```python
import math
import jax
import jax.numpy as jnp
import numpy as np
from jax import lax

D = 512
HEAD = 64
PROJ = 2048
SEQ = 256
ROWS_DEV = 256
TOK_DEV = 256
GROUP = 128
CAP = 4
BATCH = 512
ROWS = 32768


def shared_place(key):
    return jax.random.permutation(jax.random.fold_in(key, 11), ROWS).astype(jnp.int32)


def draw_row_place(key, part):
    place = shared_place(key)
    return place


def draw_item_ids(key, part):
    place = shared_place(key)
    key = jax.random.fold_in(key, 5)
    blocks = BATCH * SEQ // TOK_DEV
    keys = jax.random.split(key, 6)
    hot_owner = jax.random.randint(keys[0], (), 0, GROUP).astype(jnp.int32)
    sizes = jax.random.randint(keys[1], (blocks, GROUP), CAP // 2, CAP + 1).astype(jnp.int32)
    sizes = sizes.at[:, 0].set(CAP)
    ends = jnp.cumsum(sizes, axis=1)
    ranks = jax.vmap(lambda k: jax.random.permutation(k, TOK_DEV))(jax.random.split(keys[2], blocks)).astype(jnp.int32)
    segment = jnp.sum((ends[:, None, :] <= ranks[:, :, None]).astype(jnp.int32), axis=2)
    owner_perm = jax.vmap(lambda k: jax.random.permutation(k, GROUP))(jax.random.split(keys[3], blocks)).astype(jnp.int32)
    zero_at = jnp.argmax((owner_perm == 0).astype(jnp.int32), axis=1).astype(jnp.int32)
    column = jnp.arange(GROUP, dtype=jnp.int32)[None, :]
    moved = jnp.where(column == 0, 0, jnp.where(column == zero_at[:, None], owner_perm[:, 0:1], owner_perm))
    owner = (hot_owner + jnp.take_along_axis(moved, segment, axis=1)) % GROUP
    first = jax.random.randint(keys[4], (blocks, TOK_DEV), 0, ROWS_DEV).astype(jnp.int32)
    second = jax.random.randint(keys[5], (blocks, TOK_DEV), 0, ROWS_DEV).astype(jnp.int32)
    local_row = first * second // ROWS_DEV
    inverse = jnp.argsort(place, stable=True).astype(jnp.int32)
    ids = inverse[owner * ROWS_DEV + local_row]
    return ids.reshape(BATCH, SEQ).astype(jnp.int32)


def block_levels(key, dims, pieces, least, largest):
    loudness = 1.0
    for axis_at, shards_of in pieces:
        steps = jax.random.uniform(jax.random.fold_in(jax.random.fold_in(key, 6), axis_at), (shards_of,), jnp.float32, least / len(pieces), largest / len(pieces))
        loudness = loudness * jnp.repeat(jnp.exp(steps), dims[axis_at] // shards_of).reshape((-1,) + (1,) * (len(dims) - 1 - axis_at))
    return loudness


def profile(number_of, total, limit, slope):
    portions = [(1 << 20) // math.isqrt(rank ** slope) + 1 for rank in range(2, number_of + 1)]
    spare, counts = total - limit - (number_of - 1), [1] * (number_of - 1)
    while spare > 0:
        movable = [i for i in range(number_of - 1) if counts[i] < limit]
        pool, budget = sum([portions[i] for i in movable]), spare
        for i in movable:
            more = min(limit - counts[i], max(1, budget * portions[i] // pool), spare)
            counts[i] = counts[i] + more
            spare = spare - more
    return np.array([limit] + counts)


def uneven_parts(key, number_of, total, reach, skew):
    if number_of == 2:
        one = jax.random.randint(key, (), max(1, total - reach), min(reach, total - 1) + 1)
        return jnp.stack([one, total - one])
    sizes = jnp.asarray(profile(number_of, total, reach, skew), jnp.int32)
    twos = (number_of - 1) // 2
    donor, receiver = sizes[1:1 + 2 * twos:2], sizes[2:2 + 2 * twos:2]
    slack = jnp.minimum(donor - 1, reach - receiver)
    moved = jax.random.randint(jax.random.fold_in(key, 1), (twos,), 0, 1 << 20) % (slack + 1)
    sizes = sizes.at[1:1 + 2 * twos:2].set(donor - moved).at[2:2 + 2 * twos:2].set(receiver + moved)
    return sizes[jax.random.permutation(jax.random.fold_in(key, 2), number_of)]


def gaussian(own_key, extent, scale, most, shards=(), kind=jnp.bfloat16):
    values = jax.random.normal(own_key, extent, jnp.float32) * scale
    if len(shards) > 0:
        values = block_levels(own_key, extent, shards, -0.22, 0.18) * values
    return jnp.clip(values, min=-most, max=most).astype(kind)


def setup_inputs(seed: int = 0) -> dict:
    splits = jax.random.split(jax.random.key(seed), 7)
    history = gaussian(splits[0], (BATCH, SEQ, D), 1.0, 6.0, ((0, 512),))
    dout = gaussian(splits[1], (BATCH, SEQ, D), 1.0, 6.0, ((0, 512),))
    lengths = uneven_parts(splits[2], BATCH, BATCH * SEQ // 2, SEQ, 2).astype(jnp.int32)
    item_ids = draw_item_ids(jax.random.fold_in(splits[6], 71), 0)
    row_place = draw_row_place(jax.random.fold_in(splits[6], 71), 0)
    w1 = gaussian(splits[5], (PROJ, D), D ** -0.5, 0.25)
    return dict(history=history, dout=dout, lengths=lengths, item_ids=item_ids, row_place=row_place, w1=w1)


eps = 1e-05

def layer_norm(value):
    centred = value - lax.optimization_barrier(jnp.mean(value, axis=-1, keepdims=True))
    rstd = lax.rsqrt(lax.optimization_barrier(jnp.mean(centred * centred, axis=-1, keepdims=True)) + eps)
    return (centred * rstd, rstd)

def norm_back(grad, normed, rstd):
    return rstd * (grad - lax.optimization_barrier(jnp.mean(grad, axis=-1, keepdims=True)) - normed * lax.optimization_barrier(jnp.mean(grad * normed, axis=-1, keepdims=True)))

def user_grads(hist, cot, w1, length):
    seq = hist.shape[0]
    width = hist.shape[1]
    head = HEAD
    heads = width // head
    scale = 1.0 / head ** 0.5
    positions = jnp.arange(seq, dtype=jnp.int32)
    valid = positions < length
    inverse_len = 1.0 / length.astype(jnp.float32)
    xfull = hist.astype(jnp.float32)
    xnorm, rstd_x = layer_norm(xfull)
    xn = xnorm.astype(jnp.bfloat16)
    gates = lax.dot_general(xn, w1, (((1,), (1,)), ((), ())), preferred_element_type=jnp.float32)
    sig_g = jax.nn.sigmoid(gates)
    act = (gates * sig_g).astype(jnp.bfloat16)
    u_act = act[:, :width]
    v_act = act[:, width:2 * width].reshape(seq, heads, head)
    q_act = act[:, 2 * width:3 * width].reshape(seq, heads, head)
    k_act = act[:, 3 * width:].reshape(seq, heads, head)
    mask = ((positions[None, :] <= positions[:, None]) & valid[:, None] & valid[None, :]).astype(jnp.float32)
    scores = jnp.einsum('ihe,jhe->hij', q_act.astype(jnp.float32), k_act.astype(jnp.float32)) * scale
    sig_s = jax.nn.sigmoid(scores)
    probs = (scores * sig_s * mask * inverse_len).astype(jnp.bfloat16)
    attended = jnp.einsum('hij,jhe->ihe', probs.astype(jnp.float32), v_act.astype(jnp.float32)).reshape(seq, width)
    o_norm, rstd_o = layer_norm(attended)
    dy = cot.astype(jnp.float32) * valid[:, None].astype(jnp.float32)
    d_u = dy * o_norm
    d_on = dy * u_act.astype(jnp.float32)
    d_o = norm_back(d_on, o_norm, rstd_o).astype(jnp.bfloat16).reshape(seq, heads, head)
    d_p = jnp.einsum('ihe,jhe->hij', d_o.astype(jnp.float32), v_act.astype(jnp.float32))
    d_v = jnp.einsum('hij,ihe->jhe', probs.astype(jnp.float32), d_o.astype(jnp.float32))
    d_s = (d_p * (sig_s * (1.0 + scores * (1.0 - sig_s))) * mask * (inverse_len * scale)).astype(jnp.bfloat16)
    d_q = jnp.einsum('hij,jhe->ihe', d_s.astype(jnp.float32), k_act.astype(jnp.float32))
    d_k = jnp.einsum('hij,ihe->jhe', d_s.astype(jnp.float32), q_act.astype(jnp.float32))
    d_act = jnp.concatenate([d_u, d_v.reshape(seq, width), d_q.reshape(seq, width), d_k.reshape(seq, width)], axis=1)
    d_g = (d_act * (sig_g * (1.0 + gates * (1.0 - sig_g)))).astype(jnp.bfloat16)
    d_xn = jnp.dot(d_g, w1, preferred_element_type=jnp.float32)
    d_x = norm_back(d_xn, xnorm, rstd_x) + dy
    d_x = jnp.where(valid[:, None], d_x, 0.0).astype(jnp.bfloat16)
    return (d_x, d_g, xn)

def reference(history, dout, lengths, item_ids, row_place, w1):
    width = history.shape[2]
    total_rows = row_place.shape[0]

    def one_user(carry, inputs):
        table, weights = carry
        hist, cot, length, ids = inputs
        d_x, d_g, xn = user_grads(hist, cot, w1, length)
        places = row_place[ids].astype(jnp.int32)
        table = table.at[places].add(d_x.astype(jnp.float32))
        weights = weights + lax.dot_general(d_g, xn, (((0,), (0,)), ((), ())), preferred_element_type=jnp.float32)
        return ((table, weights), None)
    start = (jnp.zeros((total_rows, width), jnp.float32), jnp.zeros((w1.shape[0], width), jnp.float32))
    (table, weights), unused = lax.scan(one_user, start, (history, dout, lengths, item_ids))
    return (table, weights)
```

```python
import functools

import jax
import jax.numpy as jnp
from jax import lax
from jax.experimental import pallas as pl
from jax.experimental.pallas import tpu as pltpu
from jax.sharding import PartitionSpec as P

MESH = pl.DeviceIdType.MESH
F32 = jnp.float32
BF16 = jnp.bfloat16
EPS = 1e-05

SEQ = 256
D = 512
HEADS = 8
CAP = 4
NY, NX, NZ, NC = 4, 4, 16, 2

LANES = tuple((xs, cs) for xs in (0, 1, 3, 2) for cs in (0, 1))
GROUPS = ((0, 1), (1, 2), (2, 4), (4, 6), (6, 8))
STEPS_Z = tuple(sorted(range(1, NZ), key=lambda d: -min(d, NZ - d)))
STEPS_4 = (2, 1, 3)


def iota(shape, dim):
    return lax.broadcasted_iota(jnp.int32, shape, dim)


def dot_nn(a, b):
    return lax.dot_general(a, b, (((1,), (0,)), ((), ())), preferred_element_type=F32)


def dot_nt(a, b):
    return lax.dot_general(a, b, (((1,), (1,)), ((), ())), preferred_element_type=F32)


def dot_tn(a, b):
    return lax.dot_general(a, b, (((0,), (0,)), ((), ())), preferred_element_type=F32)


def silu_and_slope(value):
    sig = 0.5 * jnp.tanh(0.5 * value) + 0.5
    act = value * sig
    return act, sig + act * (1.0 - sig)


def layer_norm(value):
    centred = value - jnp.mean(value, axis=-1, keepdims=True)
    rstd = lax.rsqrt(jnp.mean(centred * centred, axis=-1, keepdims=True) + EPS)
    return centred * rstd, rstd


def norm_back(grad, normed, rstd):
    return rstd * (
        grad
        - jnp.mean(grad, axis=-1, keepdims=True)
        - normed * jnp.mean(grad * normed, axis=-1, keepdims=True)
    )


class Sems:
    def __init__(self, send, recv):
        self.send, self.recv, self.used = send, recv, 0

    def copy(self, src, dst, device):
        at = self.used
        self.used += 1
        made = pltpu.make_async_remote_copy(
            src_ref=src,
            dst_ref=dst,
            send_sem=self.send.at[at],
            recv_sem=self.recv.at[at],
            device_id=device,
            device_id_type=MESH,
        )
        made.start()
        return made


N_COPIES = 7 + 15 + 7 + 15 * len(GROUPS) + 1 + 6 + 6 + 15 + 1 + 3 + 3


def kernel(
    hist_ref, dout_ref, len_ref, ids_ref, place_ref, w1_ref,
    table_ref, weight_ref,
    xnorm, xn, act, slope, probs, sslope, attn, d_o, d_g,
    slot_s, meta_s, meta_1, meta_z, meta_2, where_s,
    out_s, lane_s, far_s, total_s, ty_s, ty_r, tg_s, tg_r,
    dw_own, dw_s, dw_r, xa_s, xa_r, xb_s, xb_r, a_own, b_own, ya_s, ya_r, yb_s, yb_r,
    zt_own, zt_s, zt_r, fin_s, fin_r,
    send, recv,
):
    y = lax.axis_index("dp")
    emb = lax.axis_index("emb")
    x = emb // (NZ * NC)
    z = lax.rem(emb // NC, NZ)
    c = lax.rem(emb, NC)

    def place(dy, dx, dz, dc):
        return (
            lax.rem(y + dy, NY),
            (lax.rem(x + dx, NX) * NZ + lax.rem(z + dz, NZ)) * NC + lax.rem(c + dc, NC),
        )

    partners = [place(0, xs, 0, cs) for xs, cs in LANES[1:]]
    partners += [place(0, 0, d, 0) for d in STEPS_Z]
    partners += [place(d, 0, 0, 0) for d in STEPS_4]
    barrier = pltpu.get_barrier_semaphore()
    for partner in partners:
        pl.semaphore_signal(barrier, inc=1, device_id=partner, device_id_type=MESH)

    sems = Sems(send, recv)
    started = []

    def remote(src, dst, device):
        made = sems.copy(src, dst, device)
        started.append(made)
        return made

    rows_i, cols_i = iota((SEQ, SEQ), 0), iota((SEQ, SEQ), 1)
    eye = rows_i == cols_i
    ids_row = ids_ref[...].astype(F32)
    ids = jnp.sum(jnp.where(eye, ids_row, 0.0), axis=1, keepdims=True).astype(jnp.int32)
    high = (cols_i == ids // 128).astype(BF16)
    lane128 = iota((SEQ, 128), 1)
    low = lane128 == lax.rem(ids, 128)
    places = place_ref[...]
    owners = dot_nn(high, (places // 256).astype(BF16))
    owner = jnp.sum(jnp.where(low, owners, 0.0), axis=1, keepdims=True).astype(jnp.int32)
    locals_ = dot_nn(high, lax.rem(places, 256).astype(BF16))
    local = jnp.sum(jnp.where(low, locals_, 0.0), axis=1, keepdims=True)
    step_x = lax.rem(owner // 32 - x + NX, NX)
    step_z = lax.rem(lax.rem(owner // 2, 16) - z + NZ, NZ)
    step_c = lax.rem(lax.rem(owner, 2) - c + NC, NC)
    order_x = jnp.where(step_x == 2, 3, jnp.where(step_x == 3, 2, step_x))
    block = ((order_x * NC + step_c) * NZ + step_z).astype(F32)
    block_row = jnp.sum(jnp.where(eye, block, 0.0), axis=0, keepdims=True)
    before = (block == block_row) & (cols_i < rows_i)
    rank = jnp.sum(jnp.where(before, 1.0, 0.0), axis=1, keepdims=True)
    slot = block * CAP + rank
    slot_s[...] = jnp.broadcast_to(jnp.sum(jnp.where(eye, slot, 0.0), axis=0, keepdims=True), (8, SEQ))
    for lane in range(8):
        wanted = (lane128 + lane * NZ * CAP).astype(F32)
        hit = (slot == wanted) & (lane128 < NZ * CAP)
        found = jnp.sum(jnp.where(hit, local - 256.0, 0.0), axis=0, keepdims=True) + 256.0
        meta = jnp.broadcast_to(found, (8, 128))
        if lane:
            meta_s[lane] = meta
        else:
            meta_1[0] = meta

    length = len_ref[...]
    inverse_len = 1.0 / length.astype(F32)
    valid = iota((SEQ, 1), 0) < length
    normed, rstd_x = layer_norm(hist_ref[0].astype(F32))
    xnorm[...] = normed
    xn[...] = normed.astype(BF16)
    for at in range(0, 4 * D, 256):
        gate = dot_nt(xn[...], w1_ref[at : at + 256, :])
        value, slant = silu_and_slope(gate)
        act[:, at : at + 256] = value.astype(BF16)
        slope[:, at : at + 256] = slant

    scale = 1.0 / 64**0.5
    mask = jnp.where((cols_i <= rows_i) & valid & (cols_i < length), inverse_len, 0.0)
    first = iota((SEQ, 128), 1) < 64
    zero = jnp.zeros((SEQ, 128), BF16)

    def split(value):
        return jnp.where(first, value, zero), jnp.where(first, zero, value)

    for pair in range(HEADS // 2):
        at = pair * 128
        v = act[:, D + at : D + at + 128]
        k = act[:, 3 * D + at : 3 * D + at + 128]
        total = None
        for half, (q, v_half) in enumerate(
            zip(split(act[:, 2 * D + at : 2 * D + at + 128]), split(v), strict=True)
        ):
            value, slant = silu_and_slope(dot_nt(q, k) * scale)
            prob = (value * mask).astype(BF16)
            probs[2 * pair + half] = prob
            sslope[2 * pair + half] = slant * (mask * scale)
            term = dot_nn(prob, v_half)
            total = term if total is None else total + term
        attn[:, at : at + 128] = total

    pl.semaphore_wait(barrier, len(partners))
    meta_copies = {
        lane: remote(meta_s.at[lane], meta_1.at[lane], place(0, xs, 0, cs))
        for lane, (xs, cs) in enumerate(LANES)
        if lane
    }

    o_norm, rstd_o = layer_norm(attn[...])
    dy = jnp.where(valid, dout_ref[0].astype(F32), 0.0)
    d_g[:, :D] = (dy * o_norm * slope[:, :D]).astype(BF16)
    d_on = dy * act[:, :D].astype(F32)
    d_o[...] = norm_back(d_on, o_norm, rstd_o).astype(BF16)

    meta_z_copies = []
    for pair in range(HEADS // 2):
        at = pair * 128
        v = act[:, D + at : D + at + 128]
        qs = split(act[:, 2 * D + at : 2 * D + at + 128])
        ks = split(act[:, 3 * D + at : 3 * D + at + 128])
        dos = split(d_o[:, at : at + 128])
        d_v = d_q = d_k = None
        for half in range(2):
            d_p = dot_nt(dos[half], v)
            d_s = (d_p * sslope[2 * pair + half]).astype(BF16)
            terms = (
                dot_tn(probs[2 * pair + half], dos[half]),
                dot_nn(d_s, ks[half]),
                dot_tn(d_s, qs[half]),
            )
            if half:
                d_v, d_q, d_k = d_v + terms[0], d_q + terms[1], d_k + terms[2]
            else:
                d_v, d_q, d_k = terms
        for part, grad in enumerate((d_v, d_q, d_k), 1):
            cols = slice(part * D + at, part * D + at + 128)
            d_g[:, cols] = (grad * slope[:, cols]).astype(BF16)
        if pair == 2:
            tile_row = iota((8, 128), 0)
            gathered = jnp.where(tile_row == 0, meta_1[0], 0.0)
            for lane, copy in meta_copies.items():
                copy.wait_recv()
                gathered += jnp.where(tile_row == lane, meta_1[lane], 0.0)
            meta_z[...] = gathered
            meta_z_copies = [remote(meta_z, meta_2.at[d], place(0, 0, d, 0)) for d in STEPS_Z]

    d_xn = dot_nn(d_g[...], w1_ref[...])
    d_x = norm_back(d_xn, xnorm[...], rstd_x) + dy
    d_x = jnp.where(valid, d_x, 0.0).astype(BF16)

    def pack(lane):
        line = iota((SEQ, SEQ), 0)
        wanted = (line // 16) * CAP + lax.rem(line, CAP) + lane * NZ * CAP
        pick = (wanted.astype(F32) == slot_s[0:1, :]).astype(BF16)
        moved = dot_nn(pick, d_x)
        quarter = lax.rem(iota((SEQ, 128), 0), 16) // CAP
        rows = moved[:, 0:128]
        for j in range(1, 4):
            rows = jnp.where(quarter == j, moved[:, 128 * j : 128 * j + 128], rows)
        return rows.astype(BF16).reshape(NZ, 16, 128)

    far_copies = [None] * len(GROUPS)

    def pass_on(group):
        low_lane, high_lane = GROUPS[group]
        far_copies[group] = [
            remote(
                lane_s.at[pl.ds(low_lane, high_lane - low_lane), d],
                far_s.at[pl.ds(low_lane, high_lane - low_lane), d],
                place(0, 0, d, 0),
            )
            for d in STEPS_Z
        ]

    lane_copies = {}
    lane_s[0] = pack(0)
    pass_on(0)
    for lane in (1, 6, 7, 2, 3, 4, 5):
        xs, cs = LANES[lane]
        out_s[lane] = pack(lane)
        lane_copies[lane] = remote(out_s.at[lane], lane_s.at[lane], place(0, xs, 0, cs))

    is_first = c == 0
    for block_at in range(8):
        share = dot_tn(d_g[:, 256 * block_at : 256 * block_at + 256], xn[...])
        left, right = share[:, :256], share[:, 256:]
        own = jnp.where(is_first, left, right)
        other = jnp.where(is_first, right, left).astype(BF16)
        for part in range(2):
            for sub in range(2):
                cut = (slice(128 * sub, 128 * sub + 128), slice(128 * part, 128 * part + 128))
                to = 2 * block_at + sub
                dw_own[part, to // 4, to % 4] = own[cut]
                dw_s[part, to // 4, to % 4] = other[cut]
    dw_copy = remote(dw_s, dw_r, place(0, 0, 0, 1))

    lane_copies[1].wait_recv()
    pass_on(1)
    for group in (2, 3, 4):
        for lane in range(*GROUPS[group]):
            lane_copies[lane].wait_recv()
        pass_on(group)

    dw_copy.wait_recv()
    for i in range(4):
        dw_own[0, i] += dw_r[0, i].astype(F32)
        xa_s[i] = dw_own[0, i].astype(BF16)
        dw_own[1, i] += dw_r[1, i].astype(F32)
        xb_s[i] = dw_own[1, i].astype(BF16)
    xa_copies = [remote(xa_s.at[:, lax.rem(x + d, NX)], xa_r.at[d - 1], place(0, d, 0, 0)) for d in STEPS_4]
    xb_copies = [remote(xb_s.at[lax.rem(y + d, NY)], xb_r.at[d - 1], place(d, 0, 0, 0)) for d in STEPS_4]

    for copy in meta_z_copies:
        copy.wait_recv()
    lane_tile = iota((8, 128), 1) // CAP
    numbers = jnp.where(lane_tile == 0, meta_z[...], 0.0)
    for d in range(1, NZ):
        numbers += jnp.where(lane_tile == d, meta_2[d], 0.0)
    numbers = jnp.where(lane_tile < NZ, numbers, 0.0).astype(BF16)
    spread_r, spread_c = iota((128, SEQ), 0), iota((128, SEQ), 1)
    spread = (spread_r // CAP == spread_c // 16) & (lax.rem(spread_r, CAP) == lax.rem(spread_c, CAP))
    where_s[...] = dot_nn(numbers, spread.astype(BF16))

    def add_rows(lane):
        hits = (rows_i.astype(F32) == where_s[lane : lane + 1, :]).astype(BF16)
        rows = jnp.concatenate([lane_s[lane, 0:1], far_s[lane, 1:NZ]], axis=0).reshape(SEQ, 128)
        quarter = lax.rem(iota((SEQ, 128), 0), 16) // CAP
        wide = jnp.concatenate([jnp.where(quarter == j, rows, zero) for j in range(4)], axis=1)
        return dot_nn(hits, wide).reshape(4, 64, D)

    def add_group(group):
        for copy in far_copies[group]:
            copy.wait_recv()
        for lane in range(*GROUPS[group]):
            if lane:
                total_s[...] += add_rows(lane)
            else:
                total_s[...] = add_rows(lane)

    add_group(0)
    add_group(1)

    for copy in (*xa_copies, *xb_copies):
        copy.wait_recv()
    a_sum = dw_own[0, :, pl.ds(x, 1)].reshape(4, 128, 128)
    b_sum = dw_own[1, pl.ds(y, 1)].reshape(4, 128, 128)
    for i in range(3):
        a_sum += xa_r[i].astype(F32)
        b_sum += xb_r[i].astype(F32)
    a_own[...] = a_sum
    b_own[...] = b_sum
    ya_s[...] = a_sum.astype(BF16)
    yb_s[...] = b_sum.astype(BF16)
    ya_copies = [remote(ya_s.at[lax.rem(y + d, NY)], ya_r.at[d - 1], place(d, 0, 0, 0)) for d in STEPS_4]
    yb_copies = [remote(yb_s.at[lax.rem(x + d, NX)], yb_r.at[d - 1], place(0, d, 0, 0)) for d in STEPS_4]

    add_group(2)

    for copy in (*ya_copies, *yb_copies):
        copy.wait_recv()
    a_end, b_end = a_own[y], b_own[x]
    for i in range(3):
        a_end += ya_r[i].astype(F32)
        b_end += yb_r[i].astype(F32)
    tiles = jnp.concatenate([a_end.reshape(NZ, 8, 128), b_end.reshape(NZ, 8, 128)], axis=1)
    zt_own[...] = tiles
    zt_s[...] = tiles.astype(BF16)

    add_group(3)
    add_group(4)

    ty_s[...] = total_s[...].astype(BF16)
    ty_copies = [remote(ty_s.at[lax.rem(y + d, NY)], ty_r.at[d - 1], place(d, 0, 0, 0)) for d in STEPS_4]
    zt_copies = [remote(zt_s.at[lax.rem(z + d, NZ)], zt_r.at[d - 1], place(0, 0, d, 0)) for d in STEPS_Z]
    for copy in ty_copies:
        copy.wait_recv()
    quarter_sum = total_s[y]
    for i in range(3):
        quarter_sum += ty_r[i].astype(F32)
    tg_s[...] = quarter_sum.astype(BF16)
    tg_copies = {d: remote(tg_s, tg_r.at[d - 1], place(d, 0, 0, 0)) for d in STEPS_4}
    table_ref[pl.ds(pl.multiple_of(y * 64, 64), 64), :] = tg_s[...].astype(F32)

    for copy in zt_copies:
        copy.wait_recv()
    tile = zt_own[z]
    for i in range(NZ - 1):
        tile += zt_r[i].astype(F32)
    fin_s[...] = tile
    fin_copy = remote(fin_s, fin_r, place(0, 0, 0, 1))

    for d, copy in tg_copies.items():
        copy.wait_recv()
        source = lax.rem(y + NY - d, NY)
        table_ref[pl.ds(pl.multiple_of(source * 64, 64), 64), :] = tg_r[d - 1].astype(F32)

    fin_copy.wait_recv()
    mine, theirs = fin_s[...], fin_r[...]
    pieces = []
    for half in range(2):
        block_half = jnp.where(is_first, mine, theirs) if half == 0 else jnp.where(is_first, theirs, mine)
        for part in range(2):
            pieces.append(
                jnp.where(is_first, block_half[8 * part : 8 * part + 4], block_half[8 * part + 4 : 8 * part + 8])
            )
    weight_ref[...] = jnp.concatenate(pieces, axis=1)

    for copy in started:
        copy.wait_send()


def body(history, dout, lengths, item_ids, row_place, w1):
    scratch = [
        pltpu.VMEM((SEQ, D), F32),
        pltpu.VMEM((SEQ, D), BF16),
        pltpu.VMEM((SEQ, 4 * D), BF16),
        pltpu.VMEM((SEQ, 4 * D), F32),
        pltpu.VMEM((HEADS, SEQ, SEQ), BF16),
        pltpu.VMEM((HEADS, SEQ, SEQ), F32),
        pltpu.VMEM((SEQ, D), F32),
        pltpu.VMEM((SEQ, D), BF16),
        pltpu.VMEM((SEQ, 4 * D), BF16),
        pltpu.VMEM((8, SEQ), F32),
        pltpu.VMEM((8, 8, 128), F32),
        pltpu.VMEM((8, 8, 128), F32),
        pltpu.VMEM((8, 128), F32),
        pltpu.VMEM((NZ, 8, 128), F32),
        pltpu.VMEM((8, SEQ), F32),
        pltpu.VMEM((8, NZ, 16, 128), BF16),
        pltpu.VMEM((8, NZ, 16, 128), BF16),
        pltpu.VMEM((8, NZ, 16, 128), BF16),
        pltpu.VMEM((4, 64, D), F32),
        pltpu.VMEM((4, 64, D), BF16),
        pltpu.VMEM((3, 64, D), BF16),
        pltpu.VMEM((64, D), BF16),
        pltpu.VMEM((3, 64, D), BF16),
        pltpu.VMEM((2, 4, 4, 128, 128), F32),
        pltpu.VMEM((2, 4, 4, 128, 128), BF16),
        pltpu.VMEM((2, 4, 4, 128, 128), BF16),
        pltpu.VMEM((4, 4, 128, 128), BF16),
        pltpu.VMEM((3, 4, 128, 128), BF16),
        pltpu.VMEM((4, 4, 128, 128), BF16),
        pltpu.VMEM((3, 4, 128, 128), BF16),
        pltpu.VMEM((4, 128, 128), F32),
        pltpu.VMEM((4, 128, 128), F32),
        pltpu.VMEM((4, 128, 128), BF16),
        pltpu.VMEM((3, 128, 128), BF16),
        pltpu.VMEM((4, 128, 128), BF16),
        pltpu.VMEM((3, 128, 128), BF16),
        pltpu.VMEM((NZ, 16, 128), F32),
        pltpu.VMEM((NZ, 16, 128), BF16),
        pltpu.VMEM((NZ - 1, 16, 128), BF16),
        pltpu.VMEM((16, 128), F32),
        pltpu.VMEM((16, 128), F32),
        pltpu.SemaphoreType.DMA((N_COPIES,)),
        pltpu.SemaphoreType.DMA((N_COPIES,)),
    ]
    vmem = pl.BlockSpec(memory_space=pltpu.VMEM)
    return pl.pallas_call(
        kernel,
        out_shape=(
            jax.ShapeDtypeStruct((SEQ, D), F32),
            jax.ShapeDtypeStruct((4, D), F32),
        ),
        in_specs=[vmem] * 6,
        out_specs=(vmem, vmem),
        scratch_shapes=scratch,
        compiler_params=pltpu.CompilerParams(
            collective_id=0, has_side_effects=True, vmem_limit_bytes=48 * 2**20
        ),
        cost_estimate=pl.CostEstimate(flops=4 * 10**9, bytes_accessed=8 * 10**6, transcendentals=10**6),
    )(history, dout, lengths.reshape(1, 1), item_ids, row_place.reshape(256, 128), w1)


def solution(mesh):
    return jax.shard_map(
        body,
        mesh=mesh,
        in_specs=(
            P(("dp", "emb"), None, None),
            P(("dp", "emb"), None, None),
            P(("dp", "emb")),
            P(("dp", "emb"), None),
            P(),
            P(),
        ),
        out_specs=(P("emb", None), P(("dp", "emb"), None)),
        check_vma=False,
    )
```

```python
import functools

import jax
import jax.numpy as jnp
from jax import lax
from jax.experimental import pallas as pl
from jax.experimental.pallas import tpu as pltpu
from jax.sharding import PartitionSpec as P

MESH = pl.DeviceIdType.MESH
F32 = jnp.float32
BF16 = jnp.bfloat16
EPS = 1e-05

SEQ = 256
D = 512
HEADS = 8
CAP = 4
NY, NX, NZ, NC = 4, 4, 16, 2

LANES = tuple((xs, cs) for xs in (0, 1, 3, 2) for cs in (0, 1))
GROUPS = ((0, 1), (1, 2), (2, 4), (4, 6), (6, 8))
NEAR = (3, -3, 2, -2, 1, -1)
RELAY = 4
STEPS_4 = (2, 1, 3)


def iota(shape, dim):
    return lax.broadcasted_iota(jnp.int32, shape, dim)


def dot_nn(a, b):
    return lax.dot_general(a, b, (((1,), (0,)), ((), ())), preferred_element_type=F32)


def dot_nt(a, b):
    return lax.dot_general(a, b, (((1,), (1,)), ((), ())), preferred_element_type=F32)


def dot_tn(a, b):
    return lax.dot_general(a, b, (((0,), (0,)), ((), ())), preferred_element_type=F32)


def silu_and_slope(value):
    sig = 0.5 * jnp.tanh(0.5 * value) + 0.5
    act = value * sig
    return act, sig + act * (1.0 - sig)


def layer_norm(value):
    centred = value - jnp.mean(value, axis=-1, keepdims=True)
    rstd = lax.rsqrt(jnp.mean(centred * centred, axis=-1, keepdims=True) + EPS)
    return centred * rstd, rstd


def norm_back(grad, normed, rstd):
    return rstd * (
        grad
        - jnp.mean(grad, axis=-1, keepdims=True)
        - normed * jnp.mean(grad * normed, axis=-1, keepdims=True)
    )


class Sems:
    def __init__(self, send, recv):
        self.send, self.recv, self.used = send, recv, 0

    def copy(self, src, dst, device):
        at = self.used
        self.used += 1
        made = pltpu.make_async_remote_copy(
            src_ref=src,
            dst_ref=dst,
            send_sem=self.send.at[at],
            recv_sem=self.recv.at[at],
            device_id=device,
            device_id_type=MESH,
        )
        made.start()
        return made


N_COPIES = 31 + 31 + 13 * len(GROUPS) + 14 + 2 + 3 + 1 + 6 + 6 + 13 + 2 + 1


def kernel(
    hist_any, dout_any, len_ref, ids_any, place_any, w1_any,
    table_ref, weight_ref,
    hist_ref, dout_ref, ids_ref, place_ref, w1_ref,
    xnorm, xn, act, slope, probs, sslope, attn, d_o, d_g,
    slot_s, meta_s, meta_1, meta_z, meta_near, meta_relay,
    out_s, lane_s, z_s, near_r, relay_r, sum_s, sum_r, tg_s, tg_r,
    dw_own, dw_s, dw_r, xa_s, xa_r, xb_s, xb_r, a_own, b_own, ya_s, ya_r, yb_s, yb_r,
    zt_own, zt_s, zt_near, zt_relay, zt_far, zt_sum_s, zt_sum_r, fin_s, fin_r,
    load, send, recv,
):
    y = lax.axis_index("dp")
    emb = lax.axis_index("emb")
    x = emb // (NZ * NC)
    z = lax.rem(emb // NC, NZ)
    c = lax.rem(emb, NC)

    def place(dy, dx, dz, dc):
        return (
            lax.rem(y + dy, NY),
            (lax.rem(x + dx, NX) * NZ + lax.rem(z + dz + NZ, NZ)) * NC + lax.rem(c + dc, NC),
        )

    partners = [place(0, 0, d, 0) for d in (RELAY, -RELAY, *NEAR)]
    partners += [place(d, xs, 0, cs) for xs, cs in LANES for d in range(NY) if d or xs or cs]
    barrier = pltpu.get_barrier_semaphore()
    for partner in partners:
        pl.semaphore_signal(barrier, inc=1, device_id=partner, device_id_type=MESH)

    sources = [(ids_any, ids_ref), (place_any, place_ref), (hist_any, hist_ref)]
    sources += [(w1_any.at[pl.ds(D * i, D)], w1_ref.at[pl.ds(D * i, D)]) for i in range(4)]
    sources += [(dout_any, dout_ref)]
    loads = [pltpu.make_async_copy(src, dst, load.at[i]) for i, (src, dst) in enumerate(sources)]
    for copy in loads:
        copy.start()

    sems = Sems(send, recv)
    started = []

    def remote(src, dst, device):
        made = sems.copy(src, dst, device)
        started.append(made)
        return made

    rows_i, cols_i = iota((SEQ, SEQ), 0), iota((SEQ, SEQ), 1)
    eye = rows_i == cols_i
    loads[0].wait()
    loads[1].wait()
    ids_row = ids_ref[...].astype(F32)
    ids = jnp.sum(jnp.where(eye, ids_row, 0.0), axis=1, keepdims=True).astype(jnp.int32)
    high = (cols_i == ids // 128).astype(BF16)
    lane128 = iota((SEQ, 128), 1)
    low = lane128 == lax.rem(ids, 128)
    places = place_ref[...]
    owners = dot_nn(high, (places // 256).astype(BF16))
    owner = jnp.sum(jnp.where(low, owners, 0.0), axis=1, keepdims=True).astype(jnp.int32)
    locals_ = dot_nn(high, lax.rem(places, 256).astype(BF16))
    local = jnp.sum(jnp.where(low, locals_, 0.0), axis=1, keepdims=True)
    step_x = lax.rem(owner // 32 - x + NX, NX)
    step_z = lax.rem(lax.rem(owner // 2, 16) - z + NZ, NZ)
    step_c = lax.rem(lax.rem(owner, 2) - c + NC, NC)
    order_x = jnp.where(step_x == 2, 3, jnp.where(step_x == 3, 2, step_x))
    block = ((order_x * NC + step_c) * NZ + step_z).astype(F32)
    block_row = jnp.sum(jnp.where(eye, block, 0.0), axis=0, keepdims=True)
    before = (block == block_row) & (cols_i < rows_i)
    rank = jnp.sum(jnp.where(before, 1.0, 0.0), axis=1, keepdims=True)
    slot = block * CAP + rank
    slot_s[...] = jnp.broadcast_to(jnp.sum(jnp.where(eye, slot, 0.0), axis=0, keepdims=True), (8, SEQ))
    for lane in range(8):
        wanted = (lane128 + lane * NZ * CAP).astype(F32)
        hit = (slot == wanted) & (lane128 < NZ * CAP)
        found = jnp.sum(jnp.where(hit, local - 256.0, 0.0), axis=0, keepdims=True) + 256.0
        meta_s[lane] = found
        if lane == 0:
            meta_1[0, 0] = found

    length = len_ref[...]
    inverse_len = 1.0 / length.astype(F32)
    valid = iota((SEQ, 1), 0) < length
    loads[2].wait()
    normed, rstd_x = layer_norm(hist_ref[0].astype(F32))
    xnorm[...] = normed
    xn[...] = normed.astype(BF16)
    for at in range(0, 4 * D, 256):
        if at % D == 0:
            loads[3 + at // D].wait()
        gate = dot_nt(xn[...], w1_ref[at : at + 256, :])
        value, slant = silu_and_slope(gate)
        act[:, at : at + 256] = value.astype(BF16)
        slope[:, at : at + 256] = slant

    scale = 1.0 / 64**0.5
    mask = jnp.where((cols_i <= rows_i) & valid & (cols_i < length), inverse_len, 0.0)
    first = iota((SEQ, 128), 1) < 64
    zero = jnp.zeros((SEQ, 128), BF16)

    def split(value):
        return jnp.where(first, value, zero), jnp.where(first, zero, value)

    for pair in range(HEADS // 2):
        at = pair * 128
        v = act[:, D + at : D + at + 128]
        k = act[:, 3 * D + at : 3 * D + at + 128]
        total = None
        for half, (q, v_half) in enumerate(
            zip(split(act[:, 2 * D + at : 2 * D + at + 128]), split(v), strict=True)
        ):
            value, slant = silu_and_slope(dot_nt(q, k) * scale)
            prob = (value * mask).astype(BF16)
            probs[2 * pair + half] = prob
            sslope[2 * pair + half] = slant * (mask * scale)
            term = dot_nn(prob, v_half)
            total = term if total is None else total + term
        attn[:, at : at + 128] = total

    o_norm, rstd_o = layer_norm(attn[...])
    loads[7].wait()
    dy = jnp.where(valid, dout_ref[0].astype(F32), 0.0)
    d_g[:, :D] = (dy * o_norm * slope[:, :D]).astype(BF16)
    d_on = dy * act[:, :D].astype(F32)
    d_o[...] = norm_back(d_on, o_norm, rstd_o).astype(BF16)

    for pair in range(HEADS // 2):
        at = pair * 128
        v = act[:, D + at : D + at + 128]
        qs = split(act[:, 2 * D + at : 2 * D + at + 128])
        ks = split(act[:, 3 * D + at : 3 * D + at + 128])
        dos = split(d_o[:, at : at + 128])
        d_v = d_q = d_k = None
        for half in range(2):
            d_p = dot_nt(dos[half], v)
            d_s = (d_p * sslope[2 * pair + half]).astype(BF16)
            terms = (
                dot_tn(probs[2 * pair + half], dos[half]),
                dot_nn(d_s, ks[half]),
                dot_tn(d_s, qs[half]),
            )
            if half:
                d_v, d_q, d_k = d_v + terms[0], d_q + terms[1], d_k + terms[2]
            else:
                d_v, d_q, d_k = terms
        for part, grad in enumerate((d_v, d_q, d_k), 1):
            cols = slice(part * D + at, part * D + at + 128)
            d_g[:, cols] = (grad * slope[:, cols]).astype(BF16)

    d_xn = dot_nn(d_g[...], w1_ref[...])
    d_x = norm_back(d_xn, xnorm[...], rstd_x) + dy
    d_x = jnp.where(valid, d_x, 0.0).astype(BF16)

    for lane in range(8):
        wanted = iota((64, SEQ), 0) + lane * NZ * CAP
        pick = (wanted.astype(F32) == slot_s[0:1, :]).astype(BF16)
        moved = dot_nn(pick, d_x).astype(BF16)
        for q in range(NY):
            out_s[lane, q] = moved[:, 128 * q : 128 * q + 128]

    pl.semaphore_wait(barrier, len(partners))
    meta_copies, lane_copies = {}, {}

    def to_lanes(*lanes):
        for lane in lanes:
            xs, cs = LANES[lane]
            meta_copies[lane], lane_copies[lane] = [], []
            for d in (2, 1, 3, 0):
                if lane or d:
                    there = place(d, xs, 0, cs)
                    meta_copies[lane].append(remote(meta_s.at[lane], meta_1.at[lane, d], there))
                    lane_copies[lane].append(remote(out_s.at[lane, lax.rem(y + d, NY)], lane_s.at[lane, d], there))

    to_lanes(*range(8))
    lane_s[0, 0] = out_s[0, y]

    to_r, from_r = iota((SEQ, SEQ), 0), iota((SEQ, SEQ), 1)
    order = (to_r // 16 == lax.rem(from_r, 64) // CAP) & (lax.rem(to_r, 16) // CAP == from_r // 64)
    order = (order & (lax.rem(to_r, CAP) == lax.rem(from_r, CAP))).astype(BF16)
    near_copies, relay_copies = [], ([], [])

    def pass_on(group):
        low, high = GROUPS[group]
        for lane in range(low, high):
            for copy in lane_copies[lane]:
                copy.wait_recv()
            rows = dot_nn(order, lane_s[lane].reshape(SEQ, 128)).astype(BF16)
            z_s[:, lane] = rows.reshape(NZ, 16, 128)
        lanes = pl.ds(low, high - low)
        way = 0 if low < 4 else 1
        ahead = (RELAY, -RELAY)[way]
        relay_copies[way].append(remote(z_s.at[8, lanes], relay_r.at[way, 3, lanes], place(0, 0, ahead, 0)))
        for d in NEAR:
            way = 0 if d > 0 else 1
            far = (d + (RELAY, -RELAY)[way]) % NZ
            relay_copies[way].append(remote(z_s.at[far, lanes], relay_r.at[way, abs(d) - 1, lanes], place(0, 0, d, 0)))
        for at, d in enumerate(NEAR):
            near_copies.append(remote(z_s.at[d % NZ, lanes], near_r.at[at, lanes], place(0, 0, d, 0)))

    is_first = c == 0

    def share_of_weight(block_at):
        share = dot_tn(d_g[:, 256 * block_at : 256 * block_at + 256], xn[...])
        left, right = share[:, :256], share[:, 256:]
        own = jnp.where(is_first, left, right)
        other = jnp.where(is_first, right, left).astype(BF16)
        for part in range(2):
            for sub in range(2):
                cut = (slice(128 * sub, 128 * sub + 128), slice(128 * part, 128 * part + 128))
                to = 2 * block_at + sub
                dw_own[part, to // 4, to % 4] = own[cut]
                dw_s[part, to // 4, to % 4] = other[cut]

    for block_at in range(4):
        share_of_weight(block_at)
    pass_on(0)
    for block_at in range(4, 8):
        share_of_weight(block_at)
    dw_copy = remote(dw_s, dw_r, place(0, 0, 0, 1))
    pass_on(1)

    for lane in range(8):
        for copy in meta_copies[lane]:
            copy.wait_recv()
    same_rank = lax.rem(iota((128, 128), 0), CAP) == lax.rem(iota((128, 128), 1), CAP)
    tall = jnp.concatenate([meta_1[lane, d] for lane in range(8) for d in range(NY)], axis=0)
    tall = jnp.broadcast_to(tall[None], (NZ, 32, 128))
    tall = jnp.where(iota((NZ, 32, 128), 2) // CAP == iota((NZ, 32, 128), 0), tall, 0.0)
    lines = dot_nn(tall.reshape(512, 128).astype(BF16), same_rank.astype(BF16)).reshape(NZ, 32, 128)
    lines = jnp.where(iota((NZ, 32, 128), 2) // CAP == iota((NZ, 32, 128), 1), lines, 0.0)
    lines = jnp.sum(lines, axis=1)
    for d in range(NZ):
        meta_z[d] = lines[d : d + 1]
    meta_z_copies = []
    for way, ahead in enumerate((RELAY, -RELAY)):
        meta_z_copies.append(remote(meta_z.at[8], meta_relay.at[way, 3], place(0, 0, ahead, 0)))
    for at, d in enumerate(NEAR):
        way = 0 if d > 0 else 1
        far = (d + (RELAY, -RELAY)[way]) % NZ
        meta_z_copies.append(remote(meta_z.at[far], meta_relay.at[way, abs(d) - 1], place(0, 0, d, 0)))
        meta_z_copies.append(remote(meta_z.at[d % NZ], meta_near.at[at], place(0, 0, d, 0)))

    for group in (2, 3, 4):
        pass_on(group)

    dw_copy.wait_recv()
    for i in range(4):
        dw_own[0, i] += dw_r[0, i].astype(F32)
        xa_s[i] = dw_own[0, i].astype(BF16)
        dw_own[1, i] += dw_r[1, i].astype(F32)
        xb_s[i] = dw_own[1, i].astype(BF16)
    xa_copies = [remote(xa_s.at[:, lax.rem(x + d, NX)], xa_r.at[d - 1], place(0, d, 0, 0)) for d in STEPS_4]
    xb_copies = [remote(xb_s.at[lax.rem(y + d, NY)], xb_r.at[d - 1], place(d, 0, 0, 0)) for d in STEPS_4]

    row_of = iota((SEQ, 128), 0).astype(F32)

    def add_up(lines_and_rows):
        hits = jnp.concatenate([(row_of == line).astype(BF16) for line, _ in lines_and_rows], axis=1)
        return dot_nn(hits, jnp.concatenate([rows for _, rows in lines_and_rows], axis=0))

    for copy in meta_z_copies:
        copy.wait_recv()
    none = jnp.zeros((64, 128), BF16)
    sum_copies = []
    for way, ahead in enumerate((RELAY, -RELAY)):
        for copy in relay_copies[way]:
            copy.wait_recv()
        half = relay_r[way, 3, 4 * way : 4 * way + 4].reshape(64, 128)
        terms = [(meta_z[ahead % NZ], z_s[ahead % NZ].reshape(128, 128))]
        terms += [(meta_relay[way, i], relay_r[way, i].reshape(128, 128)) for i in range(3)]
        terms += [(meta_relay[way, 3], jnp.concatenate([none, half] if way else [half, none], axis=0))]
        sum_s[way] = add_up(terms).astype(BF16)
        sum_copies.append(remote(sum_s.at[way], sum_r.at[way], place(0, 0, ahead, 0)))

    for copy in (*xa_copies, *xb_copies):
        copy.wait_recv()
    a_sum = dw_own[0, :, pl.ds(x, 1)].reshape(4, 128, 128)
    b_sum = dw_own[1, pl.ds(y, 1)].reshape(4, 128, 128)
    for i in range(3):
        a_sum += xa_r[i].astype(F32)
        b_sum += xb_r[i].astype(F32)
    a_own[...] = a_sum
    b_own[...] = b_sum
    ya_s[...] = a_sum.astype(BF16)
    yb_s[...] = b_sum.astype(BF16)
    ya_copies = [remote(ya_s.at[lax.rem(y + d, NY)], ya_r.at[d - 1], place(d, 0, 0, 0)) for d in STEPS_4]
    yb_copies = [remote(yb_s.at[lax.rem(x + d, NX)], yb_r.at[d - 1], place(0, d, 0, 0)) for d in STEPS_4]

    for copy in near_copies:
        copy.wait_recv()
    table = add_up(
        [(meta_z[0], z_s[0].reshape(128, 128))] + [(meta_near[i], near_r[i].reshape(128, 128)) for i in range(6)]
    )

    for copy in (*ya_copies, *yb_copies):
        copy.wait_recv()
    a_end, b_end = a_own[y], b_own[x]
    for i in range(3):
        a_end += ya_r[i].astype(F32)
        b_end += yb_r[i].astype(F32)
    tiles = jnp.concatenate([a_end.reshape(NZ, 8, 128), b_end.reshape(NZ, 8, 128)], axis=1)
    zt_own[...] = tiles
    zt_s[...] = tiles.astype(BF16)


    zt_copies = [remote(zt_s.at[lax.rem(z + 8, NZ)], zt_far, place(0, 0, RELAY + 8 * c, 0))]
    for at, d in enumerate(NEAR):
        way = 0 if d > 0 else 1
        far = (d + (RELAY, -RELAY)[way]) % NZ
        zt_copies.append(
            remote(zt_s.at[lax.rem(z + far, NZ)], zt_relay.at[way, abs(d) - 1], place(0, 0, d, 0))
        )
        zt_copies.append(remote(zt_s.at[lax.rem(z + d % NZ, NZ)], zt_near.at[at], place(0, 0, d, 0)))

    for copy in sum_copies:
        copy.wait_recv()
    tg_s[...] = (table + (sum_r[0].astype(F32) + sum_r[1].astype(F32))).astype(BF16)
    tg_copies = {d: remote(tg_s, tg_r.at[d - 1], place(d, 0, 0, 0)) for d in STEPS_4}
    table_ref[:, pl.ds(pl.multiple_of(y * 128, 128), 128)] = tg_s[...].astype(F32)

    for copy in zt_copies:
        copy.wait_recv()
    zt_sum_copies = []
    for way, ahead in enumerate((RELAY, -RELAY)):
        tile = zt_own[lax.rem(z + ahead % NZ, NZ)] + jnp.where(c == way, zt_far[...].astype(F32), 0.0)
        for i in range(3):
            tile += zt_relay[way, i].astype(F32)
        zt_sum_s[way] = tile.astype(BF16)
        zt_sum_copies.append(remote(zt_sum_s.at[way], zt_sum_r.at[way], place(0, 0, ahead, 0)))
    tile = zt_own[z]
    for i in range(6):
        tile += zt_near[i].astype(F32)

    for d, copy in tg_copies.items():
        copy.wait_recv()
        source = lax.rem(y + NY - d, NY)
        table_ref[:, pl.ds(pl.multiple_of(source * 128, 128), 128)] = tg_r[d - 1].astype(F32)

    for way, copy in enumerate(zt_sum_copies):
        copy.wait_recv()
        tile += zt_sum_r[way].astype(F32)
    fin_s[...] = tile
    fin_copy = remote(fin_s, fin_r, place(0, 0, 0, 1))
    fin_copy.wait_recv()
    mine, theirs = fin_s[...], fin_r[...]
    pieces = []
    for half in range(2):
        block_half = jnp.where(is_first, mine, theirs) if half == 0 else jnp.where(is_first, theirs, mine)
        for part in range(2):
            pieces.append(
                jnp.where(is_first, block_half[8 * part : 8 * part + 4], block_half[8 * part + 4 : 8 * part + 8])
            )
    weight_ref[...] = jnp.concatenate(pieces, axis=1)

    for copy in started:
        copy.wait_send()


def body(history, dout, lengths, item_ids, row_place, w1):
    scratch = [
        pltpu.VMEM((1, SEQ, D), BF16),
        pltpu.VMEM((1, SEQ, D), BF16),
        pltpu.VMEM((1, SEQ), jnp.int32),
        pltpu.VMEM((256, 128), jnp.int32),
        pltpu.VMEM((4 * D, D), BF16),
        pltpu.VMEM((SEQ, D), F32),
        pltpu.VMEM((SEQ, D), BF16),
        pltpu.VMEM((SEQ, 4 * D), BF16),
        pltpu.VMEM((SEQ, 4 * D), F32),
        pltpu.VMEM((HEADS, SEQ, SEQ), BF16),
        pltpu.VMEM((HEADS, SEQ, SEQ), F32),
        pltpu.VMEM((SEQ, D), F32),
        pltpu.VMEM((SEQ, D), BF16),
        pltpu.VMEM((SEQ, 4 * D), BF16),
        pltpu.VMEM((8, SEQ), F32),
        pltpu.VMEM((8, 1, 128), F32),
        pltpu.VMEM((8, NY, 1, 128), F32),
        pltpu.VMEM((NZ, 1, 128), F32),
        pltpu.VMEM((6, 1, 128), F32),
        pltpu.VMEM((2, 4, 1, 128), F32),
        pltpu.VMEM((8, NY, 64, 128), BF16),
        pltpu.VMEM((8, NY, 64, 128), BF16),
        pltpu.VMEM((NZ, 8, 16, 128), BF16),
        pltpu.VMEM((6, 8, 16, 128), BF16),
        pltpu.VMEM((2, 4, 8, 16, 128), BF16),
        pltpu.VMEM((2, SEQ, 128), BF16),
        pltpu.VMEM((2, SEQ, 128), BF16),
        pltpu.VMEM((SEQ, 128), BF16),
        pltpu.VMEM((3, SEQ, 128), BF16),
        pltpu.VMEM((2, 4, 4, 128, 128), F32),
        pltpu.VMEM((2, 4, 4, 128, 128), BF16),
        pltpu.VMEM((2, 4, 4, 128, 128), BF16),
        pltpu.VMEM((4, 4, 128, 128), BF16),
        pltpu.VMEM((3, 4, 128, 128), BF16),
        pltpu.VMEM((4, 4, 128, 128), BF16),
        pltpu.VMEM((3, 4, 128, 128), BF16),
        pltpu.VMEM((4, 128, 128), F32),
        pltpu.VMEM((4, 128, 128), F32),
        pltpu.VMEM((4, 128, 128), BF16),
        pltpu.VMEM((3, 128, 128), BF16),
        pltpu.VMEM((4, 128, 128), BF16),
        pltpu.VMEM((3, 128, 128), BF16),
        pltpu.VMEM((NZ, 16, 128), F32),
        pltpu.VMEM((NZ, 16, 128), BF16),
        pltpu.VMEM((6, 16, 128), BF16),
        pltpu.VMEM((2, 3, 16, 128), BF16),
        pltpu.VMEM((16, 128), BF16),
        pltpu.VMEM((2, 16, 128), BF16),
        pltpu.VMEM((2, 16, 128), BF16),
        pltpu.VMEM((16, 128), F32),
        pltpu.VMEM((16, 128), F32),
        pltpu.SemaphoreType.DMA((8,)),
        pltpu.SemaphoreType.DMA((N_COPIES,)),
        pltpu.SemaphoreType.DMA((N_COPIES,)),
    ]
    vmem = pl.BlockSpec(memory_space=pltpu.VMEM)
    hbm = pl.BlockSpec(memory_space=pltpu.HBM)
    return pl.pallas_call(
        kernel,
        out_shape=(
            jax.ShapeDtypeStruct((SEQ, D), F32),
            jax.ShapeDtypeStruct((4, D), F32),
        ),
        in_specs=[hbm, hbm, vmem, hbm, hbm, hbm],
        out_specs=(vmem, vmem),
        scratch_shapes=scratch,
        compiler_params=pltpu.CompilerParams(
            collective_id=0, has_side_effects=True, vmem_limit_bytes=63 * 2**20 + 2**19
        ),
        cost_estimate=pl.CostEstimate(flops=4 * 10**9, bytes_accessed=8 * 10**6, transcendentals=10**6),
    )(history, dout, lengths.reshape(1, 1), item_ids, row_place.reshape(256, 128), w1)


def solution(mesh):
    return jax.shard_map(
        body,
        mesh=mesh,
        in_specs=(
            P(("dp", "emb"), None, None),
            P(("dp", "emb"), None, None),
            P(("dp", "emb")),
            P(("dp", "emb"), None),
            P(),
            P(),
        ),
        out_specs=(P("emb", None), P(("dp", "emb"), None)),
        check_vma=False,
    )
```

```python
import functools

import jax
import jax.numpy as jnp
from jax import lax
from jax.experimental import pallas as pl
from jax.experimental.pallas import tpu as pltpu
from jax.sharding import PartitionSpec as P

MESH = pl.DeviceIdType.MESH
F32 = jnp.float32
BF16 = jnp.bfloat16
EPS = 1e-05

SEQ = 256
D = 512
HEADS = 8
CAP = 4
NY, NX, NZ, NC = 4, 4, 16, 2

LANES = tuple((xs, cs) for xs in (0, 1, 3, 2) for cs in (0, 1))
GROUPS = ((0, 1), (1, 2), (2, 4), (4, 6), (6, 8))
NEAR = (3, -3, 2, -2, 1, -1)
RELAY = 4
STEPS_4 = (2, 1, 3)


def iota(shape, dim):
    return lax.broadcasted_iota(jnp.int32, shape, dim)


def part_of(value, size):
    return lax.shift_right_logical(value, jnp.full(value.shape, size.bit_length() - 1, value.dtype))


def rest_of(value, size):
    return value & (size - 1)


def dot_nn(a, b):
    return lax.dot_general(a, b, (((1,), (0,)), ((), ())), preferred_element_type=F32)


def dot_nt(a, b):
    return lax.dot_general(a, b, (((1,), (1,)), ((), ())), preferred_element_type=F32)


def dot_tn(a, b):
    return lax.dot_general(a, b, (((0,), (0,)), ((), ())), preferred_element_type=F32)


def silu_and_slope(value):
    sig = 0.5 * jnp.tanh(0.5 * value) + 0.5
    act = value * sig
    return act, sig + act * (1.0 - sig)


def layer_norm(value):
    centred = value - jnp.mean(value, axis=-1, keepdims=True)
    rstd = lax.rsqrt(jnp.mean(centred * centred, axis=-1, keepdims=True) + EPS)
    return centred * rstd, rstd


def norm_back(grad, normed, rstd):
    return rstd * (
        grad
        - jnp.mean(grad, axis=-1, keepdims=True)
        - normed * jnp.mean(grad * normed, axis=-1, keepdims=True)
    )


class Sems:
    def __init__(self, send, recv):
        self.send, self.recv, self.used = send, recv, 0

    def copy(self, src, dst, device):
        at = self.used
        self.used += 1
        made = pltpu.make_async_remote_copy(
            src_ref=src,
            dst_ref=dst,
            send_sem=self.send.at[at],
            recv_sem=self.recv.at[at],
            device_id=device,
            device_id_type=MESH,
        )
        made.start()
        return made


N_COPIES = 31 + 31 + 13 * len(GROUPS) + 14 + 2 + 3 + 1 + 6 + 6 + 13 + 2 + 1


def kernel(
    hist_any, dout_any, len_ref, ids_any, place_any, w1_any,
    table_ref, weight_ref,
    hist_ref, dout_ref, ids_ref, place_ref, w1_ref,
    xnorm, xn, act, slope, probs, sslope, attn, d_o, d_g,
    slot_s, meta_s, meta_1, meta_z, meta_near, meta_relay,
    out_s, lane_s, z_s, near_r, relay_r, sum_s, sum_r, tg_s, tg_r,
    dw_own, dw_s, dw_r, xa_s, xa_r, xb_s, xb_r, a_own, b_own, ya_s, ya_r, yb_s, yb_r,
    zt_own, zt_s, zt_near, zt_relay, zt_far, zt_sum_s, zt_sum_r, fin_s, fin_r,
    load, send, recv,
):
    y = lax.axis_index("dp")
    emb = lax.axis_index("emb")
    x = emb // (NZ * NC)
    z = lax.rem(emb // NC, NZ)
    c = lax.rem(emb, NC)

    def place(dy, dx, dz, dc):
        return (
            lax.rem(y + dy, NY),
            (lax.rem(x + dx, NX) * NZ + lax.rem(z + dz + NZ, NZ)) * NC + lax.rem(c + dc, NC),
        )

    partners = [place(0, 0, d, 0) for d in (RELAY, -RELAY, *NEAR)]
    partners += [place(d, xs, 0, cs) for xs, cs in LANES for d in range(NY) if d or xs or cs]
    barrier = pltpu.get_barrier_semaphore()
    for partner in partners:
        pl.semaphore_signal(barrier, inc=1, device_id=partner, device_id_type=MESH)

    sources = [(hist_any, hist_ref)]
    sources += [(w1_any.at[pl.ds(D * i, D)], w1_ref.at[pl.ds(D * i, D)]) for i in range(4)]
    sources += [(ids_any, ids_ref), (place_any, place_ref), (dout_any, dout_ref)]
    loads = [pltpu.make_async_copy(src, dst, load.at[i]) for i, (src, dst) in enumerate(sources)]
    for copy in loads:
        copy.start()

    sems = Sems(send, recv)
    started = []

    def remote(src, dst, device):
        made = sems.copy(src, dst, device)
        started.append(made)
        return made

    length = len_ref[...]
    inverse_len = 1.0 / length.astype(F32)
    valid = iota((SEQ, 1), 0) < length
    loads[0].wait()
    normed, rstd_x = layer_norm(hist_ref[0].astype(F32))
    xnorm[...] = normed
    xn[...] = normed.astype(BF16)
    for at in range(0, 4 * D, 256):
        if at % D == 0:
            loads[1 + at // D].wait()
        gate = dot_nt(xn[...], w1_ref[at : at + 256, :])
        value, slant = silu_and_slope(gate)
        act[:, at : at + 256] = value.astype(BF16)
        slope[:, at : at + 256] = slant

    rows_i, cols_i = iota((SEQ, SEQ), 0), iota((SEQ, SEQ), 1)
    eye = rows_i == cols_i
    for copy in loads[5:]:
        copy.wait()
    ids_row = ids_ref[...].astype(F32)
    ids = jnp.sum(jnp.where(eye, ids_row, 0.0), axis=1, keepdims=True).astype(jnp.int32)
    high = (cols_i == part_of(ids, 128)).astype(BF16)
    lane128 = iota((SEQ, 128), 1)
    low = lane128 == rest_of(ids, 128)
    places = place_ref[...]
    owners = dot_nn(high, part_of(places, 256).astype(BF16))
    owner = jnp.sum(jnp.where(low, owners, 0.0), axis=1, keepdims=True).astype(jnp.int32)
    locals_ = dot_nn(high, rest_of(places, 256).astype(BF16))
    local = jnp.sum(jnp.where(low, locals_, 0.0), axis=1, keepdims=True)
    step_x = rest_of(part_of(owner, 32) - x + NX, NX)
    step_z = rest_of(part_of(owner, 2) - z + NZ, NZ)
    step_c = rest_of(owner - c + NC, NC)
    order_x = jnp.where(step_x == 2, 3, jnp.where(step_x == 3, 2, step_x))
    block = ((order_x * NC + step_c) * NZ + step_z).astype(F32)
    block_row = jnp.sum(jnp.where(eye, block, 0.0), axis=0, keepdims=True)
    before = (block == block_row) & (cols_i < rows_i)
    rank = jnp.sum(jnp.where(before, 1.0, 0.0), axis=1, keepdims=True)
    slot = block * CAP + rank
    slot_s[...] = jnp.broadcast_to(jnp.sum(jnp.where(eye, slot, 0.0), axis=0, keepdims=True), (8, SEQ))
    for lane in range(8):
        wanted = (lane128 + lane * NZ * CAP).astype(F32)
        hit = (slot == wanted) & (lane128 < NZ * CAP)
        found = jnp.sum(jnp.where(hit, local - 256.0, 0.0), axis=0, keepdims=True) + 256.0
        meta_s[lane] = found
        if lane == 0:
            meta_1[0, 0] = found

    scale = 1.0 / 64**0.5
    mask = jnp.where((cols_i <= rows_i) & valid & (cols_i < length), inverse_len, 0.0)
    first = iota((SEQ, 128), 1) < 64
    zero = jnp.zeros((SEQ, 128), BF16)

    def split(value):
        return jnp.where(first, value, zero), jnp.where(first, zero, value)

    for pair in range(HEADS // 2):
        at = pair * 128
        v = act[:, D + at : D + at + 128]
        k = act[:, 3 * D + at : 3 * D + at + 128]
        total = None
        for half, (q, v_half) in enumerate(
            zip(split(act[:, 2 * D + at : 2 * D + at + 128]), split(v), strict=True)
        ):
            value, slant = silu_and_slope(dot_nt(q, k) * scale)
            prob = (value * mask).astype(BF16)
            probs[2 * pair + half] = prob
            sslope[2 * pair + half] = slant * (mask * scale)
            term = dot_nn(prob, v_half)
            total = term if total is None else total + term
        attn[:, at : at + 128] = total

    o_norm, rstd_o = layer_norm(attn[...])
    dy = jnp.where(valid, dout_ref[0].astype(F32), 0.0)
    d_g[:, :D] = (dy * o_norm * slope[:, :D]).astype(BF16)
    d_on = dy * act[:, :D].astype(F32)
    d_o[...] = norm_back(d_on, o_norm, rstd_o).astype(BF16)

    for pair in range(HEADS // 2):
        at = pair * 128
        v = act[:, D + at : D + at + 128]
        qs = split(act[:, 2 * D + at : 2 * D + at + 128])
        ks = split(act[:, 3 * D + at : 3 * D + at + 128])
        dos = split(d_o[:, at : at + 128])
        d_v = d_q = d_k = None
        for half in range(2):
            d_p = dot_nt(dos[half], v)
            d_s = (d_p * sslope[2 * pair + half]).astype(BF16)
            terms = (
                dot_tn(probs[2 * pair + half], dos[half]),
                dot_nn(d_s, ks[half]),
                dot_tn(d_s, qs[half]),
            )
            if half:
                d_v, d_q, d_k = d_v + terms[0], d_q + terms[1], d_k + terms[2]
            else:
                d_v, d_q, d_k = terms
        for part, grad in enumerate((d_v, d_q, d_k), 1):
            cols = slice(part * D + at, part * D + at + 128)
            d_g[:, cols] = (grad * slope[:, cols]).astype(BF16)

    d_xn = dot_nn(d_g[...], w1_ref[...])
    d_x = norm_back(d_xn, xnorm[...], rstd_x) + dy
    d_x = jnp.where(valid, d_x, 0.0).astype(BF16)

    for lane in range(8):
        wanted = iota((64, SEQ), 0) + lane * NZ * CAP
        pick = (wanted.astype(F32) == slot_s[0:1, :]).astype(BF16)
        moved = dot_nn(pick, d_x).astype(BF16)
        for q in range(NY):
            out_s[lane, q] = moved[:, 128 * q : 128 * q + 128]

    to_r, from_r = iota((SEQ, SEQ), 0), iota((SEQ, SEQ), 1)
    order = (part_of(to_r, 16) == part_of(rest_of(from_r, 64), CAP)) & (part_of(rest_of(to_r, 16), CAP) == part_of(from_r, 64))
    order = (order & (rest_of(to_r, CAP) == rest_of(from_r, CAP))).astype(BF16)
    pl.semaphore_wait(barrier, len(partners))
    meta_copies, lane_copies = {}, {}

    def to_lanes(*lanes):
        for lane in lanes:
            xs, cs = LANES[lane]
            meta_copies[lane], lane_copies[lane] = [], []
            for d in (2, 1, 3, 0):
                if lane or d:
                    there = place(d, xs, 0, cs)
                    meta_copies[lane].append(remote(meta_s.at[lane], meta_1.at[lane, d], there))
                    lane_copies[lane].append(remote(out_s.at[lane, lax.rem(y + d, NY)], lane_s.at[lane, d], there))

    to_lanes(*range(8))
    lane_s[0, 0] = out_s[0, y]

    near_copies, relay_copies = [], ([], [])

    def pass_on(group):
        low, high = GROUPS[group]
        for lane in range(low, high):
            for copy in lane_copies[lane]:
                copy.wait_recv()
            rows = dot_nn(order, lane_s[lane].reshape(SEQ, 128)).astype(BF16)
            z_s[:, lane] = rows.reshape(NZ, 16, 128)
        lanes = pl.ds(low, high - low)
        way = 0 if low < 4 else 1
        ahead = (RELAY, -RELAY)[way]
        relay_copies[way].append(remote(z_s.at[8, lanes], relay_r.at[way, 3, lanes], place(0, 0, ahead, 0)))
        for d in NEAR:
            way = 0 if d > 0 else 1
            far = (d + (RELAY, -RELAY)[way]) % NZ
            relay_copies[way].append(remote(z_s.at[far, lanes], relay_r.at[way, abs(d) - 1, lanes], place(0, 0, d, 0)))
        for at, d in enumerate(NEAR):
            near_copies.append(remote(z_s.at[d % NZ, lanes], near_r.at[at, lanes], place(0, 0, d, 0)))

    is_first = c == 0

    def share_of_weight(block_at):
        share = dot_tn(d_g[:, 256 * block_at : 256 * block_at + 256], xn[...])
        left, right = share[:, :256], share[:, 256:]
        own = jnp.where(is_first, left, right)
        other = jnp.where(is_first, right, left).astype(BF16)
        for part in range(2):
            for sub in range(2):
                cut = (slice(128 * sub, 128 * sub + 128), slice(128 * part, 128 * part + 128))
                to = 2 * block_at + sub
                dw_own[part, to // 4, to % 4] = own[cut]
                dw_s[part, to // 4, to % 4] = other[cut]

    for block_at in range(4):
        share_of_weight(block_at)
    pass_on(0)
    for block_at in range(4, 8):
        share_of_weight(block_at)
    dw_copy = remote(dw_s, dw_r, place(0, 0, 0, 1))
    pass_on(1)

    for lane in range(8):
        for copy in meta_copies[lane]:
            copy.wait_recv()
    same_rank = rest_of(iota((128, 128), 0), CAP) == rest_of(iota((128, 128), 1), CAP)
    tall = jnp.concatenate([meta_1[lane, d] for lane in range(8) for d in range(NY)], axis=0)
    tall = jnp.broadcast_to(tall[None], (NZ, 32, 128))
    tall = jnp.where(part_of(iota((NZ, 32, 128), 2), CAP) == iota((NZ, 32, 128), 0), tall, 0.0)
    lines = dot_nn(tall.reshape(512, 128).astype(BF16), same_rank.astype(BF16)).reshape(NZ, 32, 128)
    lines = jnp.where(part_of(iota((NZ, 32, 128), 2), CAP) == iota((NZ, 32, 128), 1), lines, 0.0)
    lines = jnp.sum(lines, axis=1)
    for d in range(NZ):
        meta_z[d] = lines[d : d + 1]
    meta_z_copies = []
    for way, ahead in enumerate((RELAY, -RELAY)):
        meta_z_copies.append(remote(meta_z.at[8], meta_relay.at[way, 3], place(0, 0, ahead, 0)))
    for at, d in enumerate(NEAR):
        way = 0 if d > 0 else 1
        far = (d + (RELAY, -RELAY)[way]) % NZ
        meta_z_copies.append(remote(meta_z.at[far], meta_relay.at[way, abs(d) - 1], place(0, 0, d, 0)))
        meta_z_copies.append(remote(meta_z.at[d % NZ], meta_near.at[at], place(0, 0, d, 0)))

    for group in (2, 3, 4):
        pass_on(group)

    dw_copy.wait_recv()
    for i in range(4):
        dw_own[0, i] += dw_r[0, i].astype(F32)
        xa_s[i] = dw_own[0, i].astype(BF16)
        dw_own[1, i] += dw_r[1, i].astype(F32)
        xb_s[i] = dw_own[1, i].astype(BF16)
    xa_copies = [remote(xa_s.at[:, lax.rem(x + d, NX)], xa_r.at[d - 1], place(0, d, 0, 0)) for d in STEPS_4]
    xb_copies = [remote(xb_s.at[lax.rem(y + d, NY)], xb_r.at[d - 1], place(d, 0, 0, 0)) for d in STEPS_4]

    row_of = iota((SEQ, 128), 0).astype(F32)

    def add_up(lines_and_rows):
        hits = jnp.concatenate([(row_of == line).astype(BF16) for line, _ in lines_and_rows], axis=1)
        return dot_nn(hits, jnp.concatenate([rows for _, rows in lines_and_rows], axis=0))

    for copy in meta_z_copies:
        copy.wait_recv()
    none = jnp.zeros((64, 128), BF16)
    sum_copies = []
    for way, ahead in enumerate((RELAY, -RELAY)):
        for copy in relay_copies[way]:
            copy.wait_recv()
        half = relay_r[way, 3, 4 * way : 4 * way + 4].reshape(64, 128)
        terms = [(meta_z[ahead % NZ], z_s[ahead % NZ].reshape(128, 128))]
        terms += [(meta_relay[way, i], relay_r[way, i].reshape(128, 128)) for i in range(3)]
        terms += [(meta_relay[way, 3], jnp.concatenate([none, half] if way else [half, none], axis=0))]
        sum_s[way] = add_up(terms).astype(BF16)
        sum_copies.append(remote(sum_s.at[way], sum_r.at[way], place(0, 0, ahead, 0)))

    for copy in (*xa_copies, *xb_copies):
        copy.wait_recv()
    a_sum = dw_own[0, :, pl.ds(x, 1)].reshape(4, 128, 128)
    b_sum = dw_own[1, pl.ds(y, 1)].reshape(4, 128, 128)
    for i in range(3):
        a_sum += xa_r[i].astype(F32)
        b_sum += xb_r[i].astype(F32)
    a_own[...] = a_sum
    b_own[...] = b_sum
    ya_s[...] = a_sum.astype(BF16)
    yb_s[...] = b_sum.astype(BF16)
    ya_copies = [remote(ya_s.at[lax.rem(y + d, NY)], ya_r.at[d - 1], place(d, 0, 0, 0)) for d in STEPS_4]
    yb_copies = [remote(yb_s.at[lax.rem(x + d, NX)], yb_r.at[d - 1], place(0, d, 0, 0)) for d in STEPS_4]

    for copy in near_copies:
        copy.wait_recv()
    table = add_up(
        [(meta_z[0], z_s[0].reshape(128, 128))] + [(meta_near[i], near_r[i].reshape(128, 128)) for i in range(6)]
    )

    for copy in (*ya_copies, *yb_copies):
        copy.wait_recv()
    a_end, b_end = a_own[y], b_own[x]
    for i in range(3):
        a_end += ya_r[i].astype(F32)
        b_end += yb_r[i].astype(F32)
    tiles = jnp.concatenate([a_end.reshape(NZ, 8, 128), b_end.reshape(NZ, 8, 128)], axis=1)
    zt_own[...] = tiles
    zt_s[...] = tiles.astype(BF16)


    zt_copies = [remote(zt_s.at[lax.rem(z + 8, NZ)], zt_far, place(0, 0, RELAY + 8 * c, 0))]
    for at, d in enumerate(NEAR):
        way = 0 if d > 0 else 1
        far = (d + (RELAY, -RELAY)[way]) % NZ
        zt_copies.append(
            remote(zt_s.at[lax.rem(z + far, NZ)], zt_relay.at[way, abs(d) - 1], place(0, 0, d, 0))
        )
        zt_copies.append(remote(zt_s.at[lax.rem(z + d % NZ, NZ)], zt_near.at[at], place(0, 0, d, 0)))

    for copy in zt_copies:
        copy.wait_recv()
    zt_sum_copies = []
    for way, ahead in enumerate((RELAY, -RELAY)):
        tile = zt_own[lax.rem(z + ahead % NZ, NZ)] + jnp.where(c == way, zt_far[...].astype(F32), 0.0)
        for i in range(3):
            tile += zt_relay[way, i].astype(F32)
        zt_sum_s[way] = tile.astype(BF16)
        zt_sum_copies.append(remote(zt_sum_s.at[way], zt_sum_r.at[way], place(0, 0, ahead, 0)))
    tile = zt_own[z]
    for i in range(6):
        tile += zt_near[i].astype(F32)

    for copy in sum_copies:
        copy.wait_recv()
    tg_s[...] = (table + (sum_r[0].astype(F32) + sum_r[1].astype(F32))).astype(BF16)
    tg_copies = {d: remote(tg_s, tg_r.at[d - 1], place(d, 0, 0, 0)) for d in STEPS_4}
    table_ref[:, pl.ds(pl.multiple_of(y * 128, 128), 128)] = tg_s[...].astype(F32)

    for d, copy in tg_copies.items():
        copy.wait_recv()
        source = lax.rem(y + NY - d, NY)
        table_ref[:, pl.ds(pl.multiple_of(source * 128, 128), 128)] = tg_r[d - 1].astype(F32)

    for way, copy in enumerate(zt_sum_copies):
        copy.wait_recv()
        tile += zt_sum_r[way].astype(F32)
    fin_s[...] = tile
    fin_copy = remote(fin_s, fin_r, place(0, 0, 0, 1))
    fin_copy.wait_recv()
    mine, theirs = fin_s[...], fin_r[...]
    pieces = []
    for half in range(2):
        block_half = jnp.where(is_first, mine, theirs) if half == 0 else jnp.where(is_first, theirs, mine)
        for part in range(2):
            pieces.append(
                jnp.where(is_first, block_half[8 * part : 8 * part + 4], block_half[8 * part + 4 : 8 * part + 8])
            )
    weight_ref[...] = jnp.concatenate(pieces, axis=1)

    for copy in started:
        copy.wait_send()


def body(history, dout, lengths, item_ids, row_place, w1):
    scratch = [
        pltpu.VMEM((1, SEQ, D), BF16),
        pltpu.VMEM((1, SEQ, D), BF16),
        pltpu.VMEM((1, SEQ), jnp.int32),
        pltpu.VMEM((256, 128), jnp.int32),
        pltpu.VMEM((4 * D, D), BF16),
        pltpu.VMEM((SEQ, D), F32),
        pltpu.VMEM((SEQ, D), BF16),
        pltpu.VMEM((SEQ, 4 * D), BF16),
        pltpu.VMEM((SEQ, 4 * D), F32),
        pltpu.VMEM((HEADS, SEQ, SEQ), BF16),
        pltpu.VMEM((HEADS, SEQ, SEQ), F32),
        pltpu.VMEM((SEQ, D), F32),
        pltpu.VMEM((SEQ, D), BF16),
        pltpu.VMEM((SEQ, 4 * D), BF16),
        pltpu.VMEM((8, SEQ), F32),
        pltpu.VMEM((8, 1, 128), F32),
        pltpu.VMEM((8, NY, 1, 128), F32),
        pltpu.VMEM((NZ, 1, 128), F32),
        pltpu.VMEM((6, 1, 128), F32),
        pltpu.VMEM((2, 4, 1, 128), F32),
        pltpu.VMEM((8, NY, 64, 128), BF16),
        pltpu.VMEM((8, NY, 64, 128), BF16),
        pltpu.VMEM((NZ, 8, 16, 128), BF16),
        pltpu.VMEM((6, 8, 16, 128), BF16),
        pltpu.VMEM((2, 4, 8, 16, 128), BF16),
        pltpu.VMEM((2, SEQ, 128), BF16),
        pltpu.VMEM((2, SEQ, 128), BF16),
        pltpu.VMEM((SEQ, 128), BF16),
        pltpu.VMEM((3, SEQ, 128), BF16),
        pltpu.VMEM((2, 4, 4, 128, 128), F32),
        pltpu.VMEM((2, 4, 4, 128, 128), BF16),
        pltpu.VMEM((2, 4, 4, 128, 128), BF16),
        pltpu.VMEM((4, 4, 128, 128), BF16),
        pltpu.VMEM((3, 4, 128, 128), BF16),
        pltpu.VMEM((4, 4, 128, 128), BF16),
        pltpu.VMEM((3, 4, 128, 128), BF16),
        pltpu.VMEM((4, 128, 128), F32),
        pltpu.VMEM((4, 128, 128), F32),
        pltpu.VMEM((4, 128, 128), BF16),
        pltpu.VMEM((3, 128, 128), BF16),
        pltpu.VMEM((4, 128, 128), BF16),
        pltpu.VMEM((3, 128, 128), BF16),
        pltpu.VMEM((NZ, 16, 128), F32),
        pltpu.VMEM((NZ, 16, 128), BF16),
        pltpu.VMEM((6, 16, 128), BF16),
        pltpu.VMEM((2, 3, 16, 128), BF16),
        pltpu.VMEM((16, 128), BF16),
        pltpu.VMEM((2, 16, 128), BF16),
        pltpu.VMEM((2, 16, 128), BF16),
        pltpu.VMEM((16, 128), F32),
        pltpu.VMEM((16, 128), F32),
        pltpu.SemaphoreType.DMA((8,)),
        pltpu.SemaphoreType.DMA((N_COPIES,)),
        pltpu.SemaphoreType.DMA((N_COPIES,)),
    ]
    vmem = pl.BlockSpec(memory_space=pltpu.VMEM)
    hbm = pl.BlockSpec(memory_space=pltpu.HBM)
    return pl.pallas_call(
        kernel,
        out_shape=(
            jax.ShapeDtypeStruct((SEQ, D), F32),
            jax.ShapeDtypeStruct((4, D), F32),
        ),
        in_specs=[hbm, hbm, vmem, hbm, hbm, hbm],
        out_specs=(vmem, vmem),
        scratch_shapes=scratch,
        compiler_params=pltpu.CompilerParams(
            collective_id=0, has_side_effects=True, vmem_limit_bytes=63 * 2**20 + 2**19
        ),
        cost_estimate=pl.CostEstimate(flops=4 * 10**9, bytes_accessed=8 * 10**6, transcendentals=10**6),
    )(history, dout, lengths.reshape(1, 1), item_ids, row_place.reshape(256, 128), w1)


def solution(mesh):
    return jax.shard_map(
        body,
        mesh=mesh,
        in_specs=(
            P(("dp", "emb"), None, None),
            P(("dp", "emb"), None, None),
            P(("dp", "emb")),
            P(("dp", "emb"), None),
            P(),
            P(),
        ),
        out_specs=(P("emb", None), P(("dp", "emb"), None)),
        check_vma=False,
    )
```

```python
import functools

import jax
import jax.numpy as jnp
from jax import lax
from jax.experimental import pallas as pl
from jax.experimental.pallas import tpu as pltpu
from jax.sharding import PartitionSpec as P

MESH = pl.DeviceIdType.MESH
F32 = jnp.float32
BF16 = jnp.bfloat16
EPS = 1e-05

SEQ = 256
D = 512
HEADS = 8
CAP = 4
NY, NX, NZ, NC = 4, 4, 16, 2

LANES = tuple((xs, cs) for xs in (0, 1, 3, 2) for cs in (0, 1))
GROUPS = ((0, 1), (1, 2), (2, 4), (4, 6), (6, 8))
NEAR = (3, -3, 2, -2, 1, -1)
RELAY = 4
STEPS_4 = (2, 1, 3)


def iota(shape, dim):
    return lax.broadcasted_iota(jnp.int32, shape, dim)


def part_of(value, size):
    return lax.shift_right_logical(value, jnp.full(value.shape, size.bit_length() - 1, value.dtype))


def rest_of(value, size):
    return value & (size - 1)


def dot_nn(a, b):
    return lax.dot_general(a, b, (((1,), (0,)), ((), ())), preferred_element_type=F32)


def dot_nt(a, b):
    return lax.dot_general(a, b, (((1,), (1,)), ((), ())), preferred_element_type=F32)


def dot_tn(a, b):
    return lax.dot_general(a, b, (((0,), (0,)), ((), ())), preferred_element_type=F32)


def silu_and_slope(value):
    sig = 0.5 * jnp.tanh(0.5 * value) + 0.5
    act = value * sig
    return act, sig + act * (1.0 - sig)


def layer_norm(value):
    centred = value - jnp.mean(value, axis=-1, keepdims=True)
    rstd = lax.rsqrt(jnp.mean(centred * centred, axis=-1, keepdims=True) + EPS)
    return centred * rstd, rstd


def norm_back(grad, normed, rstd):
    return rstd * (
        grad
        - jnp.mean(grad, axis=-1, keepdims=True)
        - normed * jnp.mean(grad * normed, axis=-1, keepdims=True)
    )


class Sems:
    def __init__(self, send, recv):
        self.send, self.recv, self.used = send, recv, 0

    def copy(self, src, dst, device):
        at = self.used
        self.used += 1
        made = pltpu.make_async_remote_copy(
            src_ref=src,
            dst_ref=dst,
            send_sem=self.send.at[at],
            recv_sem=self.recv.at[at],
            device_id=device,
            device_id_type=MESH,
        )
        made.start()
        return made


N_COPIES = 31 + 31 + 13 * len(GROUPS) + 14 + 2 + 3 + 1 + 6 + 6 + 13 + 2 + 1


def kernel(
    hist_any, dout_any, len_ref, ids_any, place_any, w1_any,
    table_ref, weight_ref,
    hist_ref, dout_ref, ids_ref, place_ref, w1_ref,
    xnorm, xn, act, slope, probs, sslope, attn, d_o, d_g,
    slot_s, meta_s, meta_1, meta_z, meta_near, meta_relay,
    out_s, lane_s, z_s, near_r, relay_r, sum_s, sum_r, tg_s, tg_r,
    dw_own, dw_s, dw_r, xa_s, xa_r, xb_s, xb_r, a_own, b_own, ya_s, ya_r, yb_s, yb_r,
    zt_own, zt_s, zt_near, zt_relay, zt_far, zt_sum_s, zt_sum_r, fin_s, fin_r,
    load, send, recv,
):
    y = lax.axis_index("dp")
    emb = lax.axis_index("emb")
    x = emb // (NZ * NC)
    z = lax.rem(emb // NC, NZ)
    c = lax.rem(emb, NC)

    def place(dy, dx, dz, dc):
        return (
            lax.rem(y + dy, NY),
            (lax.rem(x + dx, NX) * NZ + lax.rem(z + dz + NZ, NZ)) * NC + lax.rem(c + dc, NC),
        )

    partners = [place(0, 0, d, 0) for d in (RELAY, -RELAY, *NEAR)]
    partners += [place(d, xs, 0, cs) for xs, cs in LANES for d in range(NY) if d or xs or cs]
    barrier = pltpu.get_barrier_semaphore()
    for partner in partners:
        pl.semaphore_signal(barrier, inc=1, device_id=partner, device_id_type=MESH)

    sources = [(hist_any, hist_ref)]
    sources += [(w1_any.at[pl.ds(D * i, D)], w1_ref.at[pl.ds(D * i, D)]) for i in range(4)]
    sources += [(ids_any, ids_ref), (place_any, place_ref), (dout_any, dout_ref)]
    loads = [pltpu.make_async_copy(src, dst, load.at[i]) for i, (src, dst) in enumerate(sources)]
    for copy in loads:
        copy.start()

    sems = Sems(send, recv)
    started = []

    def remote(src, dst, device):
        made = sems.copy(src, dst, device)
        started.append(made)
        return made

    length = len_ref[...]
    inverse_len = 1.0 / length.astype(F32)
    valid = iota((SEQ, 1), 0) < length
    loads[0].wait()
    normed, rstd_x = layer_norm(hist_ref[0].astype(F32))
    xnorm[...] = normed
    xn[...] = normed.astype(BF16)
    for at in range(0, 4 * D, 256):
        if at % D == 0:
            loads[1 + at // D].wait()
        gate = dot_nt(xn[...], w1_ref[at : at + 256, :])
        value, slant = silu_and_slope(gate)
        act[:, at : at + 256] = value.astype(BF16)
        slope[:, at : at + 256] = slant

    rows_i, cols_i = iota((SEQ, SEQ), 0), iota((SEQ, SEQ), 1)
    eye = rows_i == cols_i
    for copy in loads[5:]:
        copy.wait()
    ids_row = ids_ref[...].astype(F32)
    ids = jnp.sum(jnp.where(eye, ids_row, 0.0), axis=1, keepdims=True).astype(jnp.int32)
    high = (cols_i == part_of(ids, 128)).astype(BF16)
    lane128 = iota((SEQ, 128), 1)
    low = lane128 == rest_of(ids, 128)
    places = place_ref[...]
    owners = dot_nn(high, part_of(places, 256).astype(BF16))
    owner = jnp.sum(jnp.where(low, owners, 0.0), axis=1, keepdims=True).astype(jnp.int32)
    locals_ = dot_nn(high, rest_of(places, 256).astype(BF16))
    local = jnp.sum(jnp.where(low, locals_, 0.0), axis=1, keepdims=True)
    step_x = rest_of(part_of(owner, 32) - x + NX, NX)
    step_z = rest_of(part_of(owner, 2) - z + NZ, NZ)
    step_c = rest_of(owner - c + NC, NC)
    order_x = jnp.where(step_x == 2, 3, jnp.where(step_x == 3, 2, step_x))
    block = ((order_x * NC + step_c) * NZ + step_z).astype(F32)
    block_row = jnp.sum(jnp.where(eye, block, 0.0), axis=0, keepdims=True)
    before = (block == block_row) & (cols_i < rows_i)
    rank = jnp.sum(jnp.where(before, 1.0, 0.0), axis=1, keepdims=True)
    slot = block * CAP + rank
    slot_s[...] = jnp.broadcast_to(jnp.sum(jnp.where(eye, slot, 0.0), axis=0, keepdims=True), (8, SEQ))
    for lane in range(8):
        wanted = (lane128 + lane * NZ * CAP).astype(F32)
        hit = (slot == wanted) & (lane128 < NZ * CAP)
        found = jnp.sum(jnp.where(hit, local - 256.0, 0.0), axis=0, keepdims=True) + 256.0
        meta_s[lane] = found
        if lane == 0:
            meta_1[0, 0] = found

    scale = 1.0 / 64**0.5
    mask = jnp.where((cols_i <= rows_i) & valid & (cols_i < length), inverse_len, 0.0)
    first = iota((SEQ, 128), 1) < 64
    zero = jnp.zeros((SEQ, 128), BF16)

    def split(value):
        return jnp.where(first, value, zero), jnp.where(first, zero, value)

    for pair in range(HEADS // 2):
        at = pair * 128
        v = act[:, D + at : D + at + 128]
        k = act[:, 3 * D + at : 3 * D + at + 128]
        total = None
        for half, (q, v_half) in enumerate(
            zip(split(act[:, 2 * D + at : 2 * D + at + 128]), split(v), strict=True)
        ):
            value, slant = silu_and_slope(dot_nt(q, k) * scale)
            prob = (value * mask).astype(BF16)
            probs[2 * pair + half] = prob
            sslope[2 * pair + half] = slant * (mask * scale)
            term = dot_nn(prob, v_half)
            total = term if total is None else total + term
        attn[:, at : at + 128] = total

    o_norm, rstd_o = layer_norm(attn[...])
    dy = jnp.where(valid, dout_ref[0].astype(F32), 0.0)
    d_g[:, :D] = (dy * o_norm * slope[:, :D]).astype(BF16)
    d_on = dy * act[:, :D].astype(F32)
    d_o[...] = norm_back(d_on, o_norm, rstd_o).astype(BF16)

    for pair in range(HEADS // 2):
        at = pair * 128
        v = act[:, D + at : D + at + 128]
        qs = split(act[:, 2 * D + at : 2 * D + at + 128])
        ks = split(act[:, 3 * D + at : 3 * D + at + 128])
        dos = split(d_o[:, at : at + 128])
        d_v = d_q = d_k = None
        for half in range(2):
            d_p = dot_nt(dos[half], v)
            d_s = (d_p * sslope[2 * pair + half]).astype(BF16)
            terms = (
                dot_tn(probs[2 * pair + half], dos[half]),
                dot_nn(d_s, ks[half]),
                dot_tn(d_s, qs[half]),
            )
            if half:
                d_v, d_q, d_k = d_v + terms[0], d_q + terms[1], d_k + terms[2]
            else:
                d_v, d_q, d_k = terms
        for part, grad in enumerate((d_v, d_q, d_k), 1):
            cols = slice(part * D + at, part * D + at + 128)
            d_g[:, cols] = (grad * slope[:, cols]).astype(BF16)

    d_xn = dot_nn(d_g[...], w1_ref[...])
    d_x = norm_back(d_xn, xnorm[...], rstd_x) + dy
    d_x = jnp.where(valid, d_x, 0.0).astype(BF16)

    for lane in range(8):
        wanted = iota((64, SEQ), 0) + lane * NZ * CAP
        pick = (wanted.astype(F32) == slot_s[0:1, :]).astype(BF16)
        moved = dot_nn(pick, d_x).astype(BF16)
        for q in range(NY):
            out_s[lane, q] = moved[:, 128 * q : 128 * q + 128]

    to_r, from_r = iota((SEQ, SEQ), 0), iota((SEQ, SEQ), 1)
    order = (part_of(to_r, 16) == part_of(rest_of(from_r, 64), CAP)) & (part_of(rest_of(to_r, 16), CAP) == part_of(from_r, 64))
    order = (order & (rest_of(to_r, CAP) == rest_of(from_r, CAP))).astype(BF16)
    pl.semaphore_wait(barrier, len(partners))
    meta_copies, lane_copies = {}, {}

    def to_lanes(*lanes):
        for lane in lanes:
            xs, cs = LANES[lane]
            meta_copies[lane], lane_copies[lane] = [], []
            for d in (2, 1, 3, 0):
                if lane or d:
                    there = place(d, xs, 0, cs)
                    meta_copies[lane].append(remote(meta_s.at[lane], meta_1.at[lane, d], there))
                    lane_copies[lane].append(remote(out_s.at[lane, lax.rem(y + d, NY)], lane_s.at[lane, d], there))

    to_lanes(*range(8))
    lane_s[0, 0] = out_s[0, y]

    near_copies, relay_copies = [], ([], [])

    def pass_on(group):
        low, high = GROUPS[group]
        for lane in range(low, high):
            for copy in lane_copies[lane]:
                copy.wait_recv()
            rows = dot_nn(order, lane_s[lane].reshape(SEQ, 128)).astype(BF16)
            z_s[:, lane] = rows.reshape(NZ, 16, 128)
        lanes = pl.ds(low, high - low)
        way = 0 if low < 4 else 1
        ahead = (RELAY, -RELAY)[way]
        relay_copies[way].append(remote(z_s.at[8, lanes], relay_r.at[way, 3, lanes], place(0, 0, ahead, 0)))
        for d in NEAR:
            way = 0 if d > 0 else 1
            far = (d + (RELAY, -RELAY)[way]) % NZ
            relay_copies[way].append(remote(z_s.at[far, lanes], relay_r.at[way, abs(d) - 1, lanes], place(0, 0, d, 0)))
        for at, d in enumerate(NEAR):
            near_copies.append(remote(z_s.at[d % NZ, lanes], near_r.at[at, lanes], place(0, 0, d, 0)))

    is_first = c == 0

    def share_of_weight(block_at):
        share = dot_tn(d_g[:, 256 * block_at : 256 * block_at + 256], xn[...])
        left, right = share[:, :256], share[:, 256:]
        own = jnp.where(is_first, left, right)
        other = jnp.where(is_first, right, left).astype(BF16)
        for part in range(2):
            for sub in range(2):
                cut = (slice(128 * sub, 128 * sub + 128), slice(128 * part, 128 * part + 128))
                to = 2 * block_at + sub
                dw_own[part, to // 4, to % 4] = own[cut]
                dw_s[part, to // 4, to % 4] = other[cut]

    for block_at in range(4):
        share_of_weight(block_at)
    pass_on(0)
    for block_at in range(4, 8):
        share_of_weight(block_at)
    dw_copy = remote(dw_s, dw_r, place(0, 0, 0, 1))
    pass_on(1)

    for lane in range(8):
        for copy in meta_copies[lane]:
            copy.wait_recv()
    same_rank = rest_of(iota((128, 128), 0), CAP) == rest_of(iota((128, 128), 1), CAP)
    tall = jnp.concatenate([meta_1[lane, d] for lane in range(8) for d in range(NY)], axis=0)
    tall = jnp.broadcast_to(tall[None], (NZ, 32, 128))
    tall = jnp.where(part_of(iota((NZ, 32, 128), 2), CAP) == iota((NZ, 32, 128), 0), tall, 0.0)
    lines = dot_nn(tall.reshape(512, 128).astype(BF16), same_rank.astype(BF16)).reshape(NZ, 32, 128)
    lines = jnp.where(part_of(iota((NZ, 32, 128), 2), CAP) == iota((NZ, 32, 128), 1), lines, 0.0)
    lines = jnp.sum(lines, axis=1)
    for d in range(NZ):
        meta_z[d] = lines[d : d + 1]
    meta_z_copies = []
    for way, ahead in enumerate((RELAY, -RELAY)):
        meta_z_copies.append(remote(meta_z.at[8], meta_relay.at[way, 3], place(0, 0, ahead, 0)))
    for at, d in enumerate(NEAR):
        way = 0 if d > 0 else 1
        far = (d + (RELAY, -RELAY)[way]) % NZ
        meta_z_copies.append(remote(meta_z.at[far], meta_relay.at[way, abs(d) - 1], place(0, 0, d, 0)))
        meta_z_copies.append(remote(meta_z.at[d % NZ], meta_near.at[at], place(0, 0, d, 0)))

    for group in (2, 3, 4):
        pass_on(group)

    dw_copy.wait_recv()
    for i in range(4):
        dw_own[0, i] += dw_r[0, i].astype(F32)
        xa_s[i] = dw_own[0, i].astype(BF16)
        dw_own[1, i] += dw_r[1, i].astype(F32)
        xb_s[i] = dw_own[1, i].astype(BF16)
    xa_copies = [remote(xa_s.at[:, lax.rem(x + d, NX)], xa_r.at[d - 1], place(0, d, 0, 0)) for d in STEPS_4]
    xb_copies = [remote(xb_s.at[lax.rem(y + d, NY)], xb_r.at[d - 1], place(d, 0, 0, 0)) for d in STEPS_4]

    row_of = iota((SEQ, 128), 0).astype(F32)

    def add_up(lines_and_rows):
        hits = jnp.concatenate([(row_of == line).astype(BF16) for line, _ in lines_and_rows], axis=1)
        return dot_nn(hits, jnp.concatenate([rows for _, rows in lines_and_rows], axis=0))

    for copy in meta_z_copies:
        copy.wait_recv()
    none = jnp.zeros((64, 128), BF16)
    sum_copies = []
    for way, ahead in enumerate((RELAY, -RELAY)):
        for copy in relay_copies[way]:
            copy.wait_recv()
        half = relay_r[way, 3, 4 * way : 4 * way + 4].reshape(64, 128)
        terms = [(meta_z[ahead % NZ], z_s[ahead % NZ].reshape(128, 128))]
        terms += [(meta_relay[way, i], relay_r[way, i].reshape(128, 128)) for i in range(3)]
        terms += [(meta_relay[way, 3], jnp.concatenate([none, half] if way else [half, none], axis=0))]
        sum_s[way] = add_up(terms).astype(BF16)
        sum_copies.append(remote(sum_s.at[way], sum_r.at[way], place(0, 0, ahead, 0)))

    for copy in (*xa_copies, *xb_copies):
        copy.wait_recv()
    a_sum = dw_own[0, :, pl.ds(x, 1)].reshape(4, 128, 128)
    b_sum = dw_own[1, pl.ds(y, 1)].reshape(4, 128, 128)
    for i in range(3):
        a_sum += xa_r[i].astype(F32)
        b_sum += xb_r[i].astype(F32)
    a_own[...] = a_sum
    b_own[...] = b_sum
    ya_s[...] = a_sum.astype(BF16)
    yb_s[...] = b_sum.astype(BF16)
    ya_copies = [remote(ya_s.at[lax.rem(y + d, NY)], ya_r.at[d - 1], place(d, 0, 0, 0)) for d in STEPS_4]
    yb_copies = [remote(yb_s.at[lax.rem(x + d, NX)], yb_r.at[d - 1], place(0, d, 0, 0)) for d in STEPS_4]

    for copy in near_copies:
        copy.wait_recv()
    table = add_up(
        [(meta_z[0], z_s[0].reshape(128, 128))] + [(meta_near[i], near_r[i].reshape(128, 128)) for i in range(6)]
    )

    for copy in (*ya_copies, *yb_copies):
        copy.wait_recv()
    a_end, b_end = a_own[y], b_own[x]
    for i in range(3):
        a_end += ya_r[i].astype(F32)
        b_end += yb_r[i].astype(F32)
    tiles = jnp.concatenate([a_end.reshape(NZ, 8, 128), b_end.reshape(NZ, 8, 128)], axis=1)
    zt_own[...] = tiles
    zt_s[...] = tiles.astype(BF16)


    zt_copies = [remote(zt_s.at[lax.rem(z + 8, NZ)], zt_far, place(0, 0, RELAY + 8 * c, 0))]
    for at, d in enumerate(NEAR):
        way = 0 if d > 0 else 1
        far = (d + (RELAY, -RELAY)[way]) % NZ
        zt_copies.append(
            remote(zt_s.at[lax.rem(z + far, NZ)], zt_relay.at[way, abs(d) - 1], place(0, 0, d, 0))
        )
        zt_copies.append(remote(zt_s.at[lax.rem(z + d % NZ, NZ)], zt_near.at[at], place(0, 0, d, 0)))

    for copy in zt_copies:
        copy.wait_recv()
    zt_sum_copies = []
    for way, ahead in enumerate((RELAY, -RELAY)):
        tile = zt_own[lax.rem(z + ahead % NZ, NZ)] + jnp.where(c == way, zt_far[...].astype(F32), 0.0)
        for i in range(3):
            tile += zt_relay[way, i].astype(F32)
        zt_sum_s[way] = tile.astype(BF16)
        zt_sum_copies.append(remote(zt_sum_s.at[way], zt_sum_r.at[way], place(0, 0, ahead, 0)))
    tile = zt_own[z]
    for i in range(6):
        tile += zt_near[i].astype(F32)

    for copy in sum_copies:
        copy.wait_recv()
    tg_s[...] = (table + (sum_r[0].astype(F32) + sum_r[1].astype(F32))).astype(BF16)
    tg_copies = {d: remote(tg_s, tg_r.at[d - 1], place(d, 0, 0, 0)) for d in STEPS_4}
    table_ref[:, pl.ds(pl.multiple_of(y * 128, 128), 128)] = tg_s[...]

    for d, copy in tg_copies.items():
        copy.wait_recv()
        source = lax.rem(y + NY - d, NY)
        table_ref[:, pl.ds(pl.multiple_of(source * 128, 128), 128)] = tg_r[d - 1]

    for way, copy in enumerate(zt_sum_copies):
        copy.wait_recv()
        tile += zt_sum_r[way].astype(F32)
    fin_s[...] = tile
    fin_copy = remote(fin_s, fin_r, place(0, 0, 0, 1))
    fin_copy.wait_recv()
    mine, theirs = fin_s[...], fin_r[...]
    pieces = []
    for half in range(2):
        block_half = jnp.where(is_first, mine, theirs) if half == 0 else jnp.where(is_first, theirs, mine)
        for part in range(2):
            pieces.append(
                jnp.where(is_first, block_half[8 * part : 8 * part + 4], block_half[8 * part + 4 : 8 * part + 8])
            )
    weight_ref[...] = jnp.concatenate(pieces, axis=1)

    for copy in started:
        copy.wait_send()


def body(history, dout, lengths, item_ids, row_place, w1):
    scratch = [
        pltpu.VMEM((1, SEQ, D), BF16),
        pltpu.VMEM((1, SEQ, D), BF16),
        pltpu.VMEM((1, SEQ), jnp.int32),
        pltpu.VMEM((256, 128), jnp.int32),
        pltpu.VMEM((4 * D, D), BF16),
        pltpu.VMEM((SEQ, D), F32),
        pltpu.VMEM((SEQ, D), BF16),
        pltpu.VMEM((SEQ, 4 * D), BF16),
        pltpu.VMEM((SEQ, 4 * D), F32),
        pltpu.VMEM((HEADS, SEQ, SEQ), BF16),
        pltpu.VMEM((HEADS, SEQ, SEQ), F32),
        pltpu.VMEM((SEQ, D), F32),
        pltpu.VMEM((SEQ, D), BF16),
        pltpu.VMEM((SEQ, 4 * D), BF16),
        pltpu.VMEM((8, SEQ), F32),
        pltpu.VMEM((8, 1, 128), F32),
        pltpu.VMEM((8, NY, 1, 128), F32),
        pltpu.VMEM((NZ, 1, 128), F32),
        pltpu.VMEM((6, 1, 128), F32),
        pltpu.VMEM((2, 4, 1, 128), F32),
        pltpu.VMEM((8, NY, 64, 128), BF16),
        pltpu.VMEM((8, NY, 64, 128), BF16),
        pltpu.VMEM((NZ, 8, 16, 128), BF16),
        pltpu.VMEM((6, 8, 16, 128), BF16),
        pltpu.VMEM((2, 4, 8, 16, 128), BF16),
        pltpu.VMEM((2, SEQ, 128), BF16),
        pltpu.VMEM((2, SEQ, 128), BF16),
        pltpu.VMEM((SEQ, 128), BF16),
        pltpu.VMEM((3, SEQ, 128), BF16),
        pltpu.VMEM((2, 4, 4, 128, 128), F32),
        pltpu.VMEM((2, 4, 4, 128, 128), BF16),
        pltpu.VMEM((2, 4, 4, 128, 128), BF16),
        pltpu.VMEM((4, 4, 128, 128), BF16),
        pltpu.VMEM((3, 4, 128, 128), BF16),
        pltpu.VMEM((4, 4, 128, 128), BF16),
        pltpu.VMEM((3, 4, 128, 128), BF16),
        pltpu.VMEM((4, 128, 128), F32),
        pltpu.VMEM((4, 128, 128), F32),
        pltpu.VMEM((4, 128, 128), BF16),
        pltpu.VMEM((3, 128, 128), BF16),
        pltpu.VMEM((4, 128, 128), BF16),
        pltpu.VMEM((3, 128, 128), BF16),
        pltpu.VMEM((NZ, 16, 128), F32),
        pltpu.VMEM((NZ, 16, 128), BF16),
        pltpu.VMEM((6, 16, 128), BF16),
        pltpu.VMEM((2, 3, 16, 128), BF16),
        pltpu.VMEM((16, 128), BF16),
        pltpu.VMEM((2, 16, 128), BF16),
        pltpu.VMEM((2, 16, 128), BF16),
        pltpu.VMEM((16, 128), F32),
        pltpu.VMEM((16, 128), F32),
        pltpu.SemaphoreType.DMA((8,)),
        pltpu.SemaphoreType.DMA((N_COPIES,)),
        pltpu.SemaphoreType.DMA((N_COPIES,)),
    ]
    vmem = pl.BlockSpec(memory_space=pltpu.VMEM)
    hbm = pl.BlockSpec(memory_space=pltpu.HBM)
    table, weight = pl.pallas_call(
        kernel,
        out_shape=(
            jax.ShapeDtypeStruct((SEQ, D), BF16),
            jax.ShapeDtypeStruct((4, D), F32),
        ),
        in_specs=[hbm, hbm, vmem, hbm, hbm, hbm],
        out_specs=(vmem, vmem),
        scratch_shapes=scratch,
        compiler_params=pltpu.CompilerParams(
            collective_id=0, has_side_effects=True, vmem_limit_bytes=63 * 2**20 + 2**19
        ),
        cost_estimate=pl.CostEstimate(flops=4 * 10**9, bytes_accessed=8 * 10**6, transcendentals=10**6),
    )(history, dout, lengths.reshape(1, 1), item_ids, row_place.reshape(256, 128), w1)
    return table.astype(F32), weight


def solution(mesh):
    return jax.shard_map(
        body,
        mesh=mesh,
        in_specs=(
            P(("dp", "emb"), None, None),
            P(("dp", "emb"), None, None),
            P(("dp", "emb")),
            P(("dp", "emb"), None),
            P(),
            P(),
        ),
        out_specs=(P("emb", None), P(("dp", "emb"), None)),
        check_vma=False,
    )
```
